32 devices in a mesh: gx: 8 (over y, x, core), gy: 4 (over z).
Axes of the slice: x: 2, y: 2, z: 4, core: 2. Of those that a mesh axis runs over, the one named last changes fastest.
Arguments:
- body_force: float32 [3, 256, 128, 128], P(None, 'gx', 'gy'), may hold values from -8 to 8
- shift_coef: float32 [256, 128, 128], P('gx', 'gy'), may hold values from 0.25 to 2
- coupling: float32 [7776, 1024], P(None, ('gx', 'gy')), may hold values from -0.625 to 0.625
- node_cells: int32 [32, 1024], P(None, ('gx', 'gy')), may hold values from 0 to 131071
- target_gap: float32 [81, 1024], P(None, ('gx', 'gy')), may hold values from -4 to 4
- new_owner: int32 [1024, 1], P(('gx', 'gy')), may hold values from 0 to 7; in each aligned block of 32 rows (0 to 31, 32 to 63, ...) at most 4 rows name the same one
Outputs:
- multipliers: float32 [81, 1024], P(None, ('gx', 'gy'))
- velocity: float32 [3, 256, 128, 128], P(None, 'gx', 'gy')
The draws below stay inside these ranges and needn't reach their ends.
Inputs may be any that keep to these rules, and one draw needn't show every extreme that they name: `new_owner`: among the 32 elements of one device, at most 4 name the same new owner, and exactly 4 do for some owner.
All inputs are finite; a program needn't handle non-finite values.
Results may differ from the reference program's by a relative error of at most 0.0003.
Values sent between devices are 32-bit elements; how exact they have to be, the bound alone decides.
A program may use at most 64 MiB of HBM per device.

```python
import math
import jax
import jax.numpy as jnp
import numpy as np
from jax import lax

CX = 32
CY = 32
CZ = 128
E_DEV = 32
COMP = 3
NODES = 32
MULT = 81
ITERS = 4
CAP = 4
NX = 256
NY = 128
NZ = 128
E = 1024
N_GX = 8
N_GY = 4


def with_ends(drawn, rng, smallest, high):
    index_at = [jax.random.randint(jax.random.fold_in(rng, axis), (), 0, length) for axis, length in enumerate(drawn.shape)]
    main_axis = drawn.shape.index(max(drawn.shape))
    next_to = index_at[:main_axis] + [(index_at[main_axis] + 1) % drawn.shape[main_axis]] + index_at[main_axis + 1:]
    return drawn.at[tuple(index_at)].set(smallest).at[tuple(next_to)].set(high)


def block_levels(key, shape, cuts, low, largest):
    loudness = 1.0
    for position, blocks in cuts:
        heights = jax.random.uniform(jax.random.fold_in(jax.random.fold_in(key, 6), position), (blocks,), jnp.float32, low / len(cuts), largest / len(cuts))
        loudness = loudness * jnp.repeat(jnp.exp(heights), shape[position] // blocks).reshape((-1,) + (1,) * (len(shape) - 1 - position))
    return loudness


def shared_out(key, own, number, rows, amount, top, bound, lean):
    sequence = jax.random.permutation(key, amount)
    packed, usual = portions_of(amount, rows * top, bound, lean, True), portions_of(amount, rows * top, bound, lean, False)
    places = jnp.arange(amount)

    def named(sizes, rotation):
        used = int((sizes > 0).sum())
        fixed = max(1, used // 4)
        moved = fixed + (places - fixed + rotation * (used - fixed)) % max(1, amount - fixed)
        return jnp.zeros((amount,), jnp.int32).at[sequence[jnp.where(places < fixed, places, moved)]].set(jnp.asarray(sizes, jnp.int32))

    sizes = jnp.where(number % 4 == 0, named(packed, number // 4), named(usual, number - number // 4 - 1))
    mixed = jax.random.permutation(jax.random.fold_in(own, 3), amount)
    giver, taker = mixed[0:amount // 2 * 2:2], mixed[1:amount // 2 * 2:2]
    slack = jnp.minimum(sizes[giver] - 1, bound - sizes[taker]) // 2
    slack = jnp.where((giver == sequence[0]) | (taker == sequence[0]) | (sizes[taker] == 0), 0, jnp.maximum(slack, 0))
    moved = jax.random.randint(jax.random.fold_in(own, 4), (amount // 2,), 0, 1 << 20) % (slack + 1)
    sizes = sizes.at[giver].add(-moved).at[taker].add(moved)
    items = jnp.searchsorted(jnp.cumsum(sizes), jnp.arange(rows * top), side="right").astype(jnp.int32)
    table = items.reshape(top, rows).T
    table = table[jax.random.permutation(jax.random.fold_in(own, 1), rows)]
    rotation = jax.random.randint(jax.random.fold_in(own, 2), (rows, 1), 0, top)
    return jnp.take_along_axis(table, (jnp.arange(top)[None, :] + rotation) % top, axis=1)


def portions_of(number_of, total, most, slope, full):
    portions = [(1 << 20) // math.isqrt(standing ** slope) + 1 for standing in range(1, number_of + 1)]
    largest = most if full else min(most, max(-(-total // number_of), total * portions[0] // sum(portions)))
    least = 1 if total - largest >= number_of - 1 else 0
    given, rest = [largest] + [least] * (number_of - 1), total - largest - least * (number_of - 1)
    while rest > 0:
        movable = [i for i in range(1, number_of) if given[i] < largest] or [i for i in range(1, number_of) if given[i] < most]
        pool, left = sum([portions[i] for i in movable]), rest
        for i in movable:
            addition = min(most - given[i], max(1, left * portions[i] // pool), rest)
            given[i] = given[i] + addition
            rest = rest - addition
    return np.array(given)


def noise(own_key, shape, spread, most, split=(), held_as=jnp.bfloat16):
    factor_of = block_levels(own_key, shape, split, -0.22, 0.18) if split else 1.0
    array = jax.random.normal(own_key, shape, jnp.float32) * spread * factor_of
    return jnp.minimum(jnp.maximum(array, -most), most).astype(held_as)


def setup_inputs(seed: int = 0) -> dict:
    streams_of = jax.random.split(jax.random.key(seed), 7)
    body_force = noise(streams_of[0], (COMP, NX, NY, NZ), 1.0, 8.0, ((1, 8), (2, 4)), jnp.float32)
    shift_coef = jnp.clip(0.25 + 1.75 * jax.random.uniform(streams_of[1], (NX, NY, NZ), jnp.float32) ** block_levels(streams_of[1], (NX, NY, NZ), ((0, 8), (1, 4)), -0.2, 0.2), 0.25, 2.0)
    coupling = noise(streams_of[2], (COMP * NODES * MULT, E), (COMP * NODES) ** -0.5, 0.625, ((1, 32),), jnp.float32)
    node_cells = with_ends(jax.random.randint(streams_of[3], (NODES, E), 0, CX * CY * CZ), jax.random.fold_in(streams_of[3], 1), 0, (CX * CY * CZ) - 1).astype(jnp.int32)
    target_gap = noise(streams_of[4], (MULT, E), 0.3, 4.0, ((1, 32),), jnp.float32)
    new_owner_keys = jax.random.split(jax.random.fold_in(streams_of[5], 1), E // E_DEV)
    new_owner_turns = jax.random.permutation(jax.random.fold_in(streams_of[5], 3), E // E_DEV)
    new_owner = jax.vmap(lambda own, number: shared_out(jax.random.fold_in(streams_of[5], 2), own, number, E_DEV, N_GX, 1, CAP, 2))(new_owner_keys, new_owner_turns).reshape((E, 1))
    return dict(body_force=body_force, shift_coef=shift_coef, coupling=coupling, node_cells=node_cells, target_gap=target_gap, new_owner=new_owner)


def operate(fluid_field, shift_coef):
    padded = jnp.pad(fluid_field, ((0, 0), (1, 1), (1, 1), (1, 1)))
    beside = padded[:, 2:, 1:-1, 1:-1] + padded[:, :-2, 1:-1, 1:-1]
    beside = beside + padded[:, 1:-1, 2:, 1:-1] + padded[:, 1:-1, :-2, 1:-1]
    beside = beside + padded[:, 1:-1, 1:-1, 2:] + padded[:, 1:-1, 1:-1, :-2]
    return (6.0 + shift_coef) * fluid_field - beside


def smooth(residual_in, shift_coef):
    diagonal = 6.0 + shift_coef
    first_pass = residual_in / diagonal
    return first_pass + (residual_in - operate(first_pass, shift_coef)) / diagonal


def reference(body_force, shift_coef, coupling, node_cells, target_gap, new_owner):
    elems = jnp.arange(E, dtype=jnp.int32)
    row_index = (elems // E_DEV) % N_GY
    owners = new_owner[:, 0].astype(jnp.int32)
    pos_first = owners[None, :] * CX + node_cells // (CY * CZ)
    pos_second = row_index[None, :] * CY + (node_cells // CZ) % CY
    pos_third = node_cells % CZ
    flat_cell = (pos_first * NY + pos_second) * NZ + pos_third
    cell_count = NX * NY * NZ
    dof_index = (jnp.arange(COMP, dtype=jnp.int32)[:, None, None] * cell_count + flat_cell[None]).reshape(COMP * NODES, E)
    blocks = coupling.reshape(COMP * NODES, MULT, E)

    def apply_b(fluid_field):
        values = fluid_field.reshape(-1)[dof_index]
        return jnp.einsum("ame,ae->me", blocks, values, precision=lax.Precision.HIGHEST)

    def apply_bt(multi):
        term_cols = jnp.einsum("ame,me->ae", blocks, multi, precision=lax.Precision.HIGHEST)
        flat = jnp.zeros((COMP * cell_count,), jnp.float32).at[dof_index.reshape(-1)].add(term_cols.reshape(-1))
        return flat.reshape(body_force.shape)

    goal_vals = apply_b(smooth(body_force, shift_coef)) - target_gap
    multipliers = jnp.zeros_like(goal_vals)
    residual = goal_vals
    direction = goal_vals
    norm_now = jnp.sum(residual * residual)
    for iteration in range(ITERS):
        image = apply_b(smooth(apply_bt(direction), shift_coef))
        step_size = norm_now / jnp.sum(direction * image)
        multipliers = multipliers + step_size * direction
        residual = residual - step_size * image
        norm_next = jnp.sum(residual * residual)
        direction = residual + (norm_next / norm_now) * direction
        norm_now = norm_next
    velocity = smooth(body_force - apply_bt(multipliers), shift_coef)
    return multipliers, velocity
```

```python
import functools
import jax
import jax.numpy as jnp
from jax import lax
from jax.experimental import pallas as pl
from jax.experimental.pallas import tpu as pltpu
from jax.sharding import PartitionSpec as P

COMP = 3
NODES = 32
MULT = 81
ITERS = 4
CAP = 4
ROWS = 88
MESH = pl.DeviceIdType.MESH


def pieces(values):
    high = values.astype(jnp.bfloat16).astype(jnp.float32)
    return jnp.concatenate([high, values - high], axis=0).astype(jnp.bfloat16)


def uzawa_kernel(ngx, ngy, slots, strides, spans, row_ref, col_ref, inv_ref, block_ref, goal_ref,
                 mult_ref, out_ref, links, sent, got, part, line, total, far, swap_sem, line_sem, far_sem):
    me_x, me_y = lax.axis_index("gx"), lax.axis_index("gy")
    nodes = row_ref.shape[1]
    quads = nodes // 128
    z_step, x_step = strides
    x_span, y_span = spans

    barrier = pltpu.get_barrier_semaphore()
    for o in range(1, ngx):
        pl.semaphore_signal(barrier, inc=1, device_id={"gx": lax.rem(me_x + o, ngx)}, device_id_type=MESH)
    for o in range(1, ngy):
        pl.semaphore_signal(barrier, inc=1, device_id={"gy": lax.rem(me_y + o, ngy)}, device_id_type=MESH)
    pl.semaphore_wait(barrier, ngx + ngy - 2)

    def exchange(source, slot):
        copies = []
        for side, (axis, me, count, step) in enumerate(
            (("gx", me_x, ngx, 1), ("gx", me_x, ngx, ngx - 1), ("gy", me_y, ngy, 1), ("gy", me_y, ngy, ngy - 1))
        ):
            copy = pltpu.make_async_remote_copy(
                src_ref=source, dst_ref=got.at[slot, side],
                send_sem=swap_sem.at[0, slot, side], recv_sem=swap_sem.at[1, slot, side],
                device_id={axis: lax.rem(me + step, count)}, device_id_type=MESH)
            copy.start()
            copies.append(copy)
        return copies

    copies = exchange(row_ref, 0)
    tile = 128

    @pl.loop(0, nodes // tile)
    def _(i):
        at = pl.ds(pl.multiple_of(i * tile, tile), tile)
        gap = jnp.abs(row_ref[0:1, :] - col_ref[at, :])
        links[0, at, :] = jnp.where(gap == 0.0, 1.0, 0.0).astype(jnp.bfloat16)
        links[1, at, :] = jnp.where(
            (gap == 1.0) | (gap == z_step) | (gap == x_step), 1.0, 0.0).astype(jnp.bfloat16)

    for copy in copies:
        copy.wait()
    nowhere = jnp.float32(8.0 * (x_span + x_step))
    from_left = jnp.where(me_x > 0, x_step - x_span, nowhere).astype(jnp.float32)
    from_right = jnp.where(me_x < ngx - 1, x_span - x_step, nowhere).astype(jnp.float32)
    from_below = jnp.where(me_y > 0, z_step - y_span, nowhere).astype(jnp.float32)
    from_above = jnp.where(me_y < ngy - 1, y_span - z_step, nowhere).astype(jnp.float32)

    @pl.loop(0, nodes // tile)
    def _(i):
        at = pl.ds(pl.multiple_of(i * tile, tile), tile)
        own = col_ref[at, :]
        for side, offset in enumerate((from_left, from_right, from_below, from_above)):
            moved = got[0, side, 0:1, :] + offset
            links[2 + side, at, :] = jnp.where(moved == own, 1.0, 0.0).astype(jnp.bfloat16)

    def apply_link(kind, values):
        both = lax.dot_general(
            pieces(values), links[kind], (((1,), (1,)), ((), ())), preferred_element_type=jnp.float32)
        return both[0:8] + both[8:16]

    def apply_bt(multi, into):
        for c in range(COMP):
            for q in range(quads):
                into[c:c + 1, q * 128:(q + 1) * 128] = jnp.sum(
                    block_ref[c * quads + q] * multi, axis=0, keepdims=True)

    def apply_b(values):
        image = jnp.zeros((ROWS, 128), jnp.float32)
        for c in range(COMP):
            for q in range(quads):
                image = image + block_ref[c * quads + q] * values[c:c + 1, q * 128:(q + 1) * 128]
        shift = 64
        while shift >= slots:
            image = image + pltpu.roll(image, shift, 1)
            shift //= 2
        return image

    def all_sum(slot):
        for axis, me, count, source, room, sems in (
            ("gx", me_x, ngx, part, line, line_sem), ("gy", me_y, ngy, total, far, far_sem)):
            copies = []
            for o in range(1, count):
                copy = pltpu.make_async_remote_copy(
                    src_ref=source, dst_ref=room.at[slot, o],
                    send_sem=sems.at[0, slot, o], recv_sem=sems.at[1, slot, o],
                    device_id={axis: lax.rem(me + o, count)}, device_id_type=MESH)
                copy.start()
                copies.append(copy)
            summed = source[...]
            for o, copy in enumerate(copies):
                copy.wait()
                summed = summed + room[slot, o + 1]
            if axis == "gx":
                total[...] = summed
        return summed

    sent[...] = jnp.zeros_like(sent)
    part[...] = jnp.zeros_like(part)
    inverse = inv_ref[...]

    def step(iteration, state):
        multi, residual, direction = state
        apply_bt(direction, sent)
        scaled = sent[...] * inverse
        sent[...] = scaled
        copies = exchange(sent, iteration + 1)
        here = apply_link(0, scaled)
        beside = apply_link(1, scaled)
        for side, copy in enumerate(copies):
            copy.wait()
            beside = beside + apply_link(2 + side, got[iteration + 1, side])
        image = apply_b(here + beside * inverse)
        for row, (a, b) in enumerate(
            ((residual, residual), (direction, image), (residual, image), (image, image))):
            part[row:row + 1, :] = jnp.sum(a * b, axis=0, keepdims=True)
        sums = jnp.sum(all_sum(iteration), axis=1, keepdims=True)
        norm_now, bend, cross, square = sums[0:1], sums[1:2], sums[2:3], sums[3:4]
        step_size = norm_now / bend
        norm_next = norm_now - 2.0 * step_size * cross + step_size * step_size * square
        multi = multi + step_size * direction
        residual = residual - step_size * image
        direction = residual + norm_next / norm_now * direction
        return multi, residual, direction

    goal = goal_ref[...]
    multi, _, _ = lax.fori_loop(0, ITERS, step, (jnp.zeros_like(goal), goal, goal))
    mult_ref[...] = multi
    out_ref[...] = jnp.zeros_like(out_ref)
    apply_bt(multi, out_ref)


def smooth(residual_in, shift_coef):
    inverse = 1.0 / (6.0 + shift_coef)
    first_pass = residual_in * inverse
    count_x, count_y = lax.axis_size("gx"), lax.axis_size("gy")

    def halo(axis, dim, count):
        head = lax.slice_in_dim(first_pass, 0, 1, axis=dim)
        tail = lax.slice_in_dim(first_pass, first_pass.shape[dim] - 1, first_pass.shape[dim], axis=dim)
        before = lax.ppermute(tail, axis, [(i, i + 1) for i in range(count - 1)])
        after = lax.ppermute(head, axis, [(i + 1, i) for i in range(count - 1)])
        grown = jnp.concatenate([before, first_pass, after], axis=dim)
        size = first_pass.shape[dim]
        return lax.slice_in_dim(grown, 0, size, axis=dim) + lax.slice_in_dim(grown, 2, size + 2, axis=dim)

    beside = halo("gx", 1, count_x) + halo("gy", 2, count_y)
    wide = jnp.pad(first_pass, ((0, 0), (0, 0), (0, 0), (1, 1)))
    beside = beside + wide[..., 2:] + wide[..., :-2]
    return first_pass + beside * inverse


def shards(body_force, shift_coef, coupling, node_cells, target_gap, new_owner):
    groups, rows_gy = lax.axis_size("gx"), lax.axis_size("gy")
    slots = groups * CAP
    pack = 128 // slots
    quads = NODES // pack
    nodes = NODES * slots
    owners = new_owner[:, 0]
    onehot = (owners[:, None] == jnp.arange(groups, dtype=jnp.int32)[None, :]).astype(jnp.int32)
    rank_in = jnp.sum((jnp.cumsum(onehot, axis=0) - 1) * onehot, axis=1)
    slot_of = owners * CAP + rank_in
    _, cx, cy, cz = body_force.shape
    cell_total = cx * cy * cz

    held = jnp.concatenate([coupling, node_cells.astype(jnp.float32), target_gap], axis=0)
    choose = (slot_of[:, None] == jnp.arange(slots, dtype=jnp.int32)[None, :]).astype(jnp.float32)
    held = jnp.dot(held, choose, precision=lax.Precision.HIGHEST)
    moved = lax.all_to_all(held, "gx", split_axis=1, concat_axis=1, tiled=True)
    block_rows = COMP * NODES * MULT
    blocks = moved[:block_rows].reshape(COMP * quads, pack, MULT, slots)
    blocks = jnp.pad(blocks.transpose(0, 2, 1, 3).reshape(COMP * quads, MULT, 128), ((0, 0), (0, ROWS - MULT), (0, 0)))
    cell_int = jnp.round(moved[block_rows:block_rows + NODES]).astype(jnp.int32).reshape(nodes)
    gap = moved[block_rows + NODES:]

    z_step = cz + 2
    x_step = z_step * (3 * cy + 4)
    ids = (cell_int // (cy * cz) * x_step + cell_int // cz % cy * z_step + cell_int % cz).astype(jnp.float32)
    dof_index = jnp.arange(COMP, dtype=jnp.int32)[:, None] * cell_total + cell_int[None]
    start = smooth(body_force, shift_coef).reshape(-1)[dof_index].reshape(COMP * quads, 128)
    image = jnp.sum(blocks * start[:, None, :], axis=0)
    image = jnp.sum(image.reshape(ROWS, pack, slots), axis=1)
    goal = jnp.tile(image - jnp.pad(gap, ((0, ROWS - MULT), (0, 0))), (1, pack))
    inverse = 1.0 / (6.0 + shift_coef.reshape(-1)[cell_int])

    vmem = pl.BlockSpec(memory_space=pltpu.VMEM)
    multi, force = pl.pallas_call(
        functools.partial(
            uzawa_kernel, groups, rows_gy, slots, (float(z_step), float(x_step)),
            (float(cx * x_step), float(cy * z_step))),
        out_shape=(
            jax.ShapeDtypeStruct((ROWS, 128), jnp.float32),
            jax.ShapeDtypeStruct((8, nodes), jnp.float32),
        ),
        in_specs=[vmem] * 5,
        out_specs=(vmem, vmem),
        scratch_shapes=[
            pltpu.VMEM((6, nodes, nodes), jnp.bfloat16),
            pltpu.VMEM((8, nodes), jnp.float32),
            pltpu.VMEM((ITERS + 1, 4, 8, nodes), jnp.float32),
            pltpu.VMEM((8, 128), jnp.float32),
            pltpu.VMEM((ITERS, groups, 8, 128), jnp.float32),
            pltpu.VMEM((8, 128), jnp.float32),
            pltpu.VMEM((ITERS, rows_gy, 8, 128), jnp.float32),
            pltpu.SemaphoreType.DMA((2, ITERS + 1, 4)),
            pltpu.SemaphoreType.DMA((2, ITERS, groups)),
            pltpu.SemaphoreType.DMA((2, ITERS, rows_gy)),
        ],
        compiler_params=pltpu.CompilerParams(
            collective_id=0, has_side_effects=True,
            vmem_limit_bytes=(12 * nodes * nodes + (12 << 20))),
    )(
        jnp.broadcast_to(ids[None], (8, nodes)), ids[:, None],
        jnp.broadcast_to(inverse[None], (8, nodes)), blocks, goal,
    )

    flat = jnp.zeros((COMP * cell_total,), jnp.float32).at[dof_index.reshape(-1)].add(force[:COMP].reshape(-1))
    velocity = smooth(body_force - flat.reshape(body_force.shape), shift_coef)
    back = lax.all_to_all(multi[:MULT, :slots], "gx", split_axis=1, concat_axis=1, tiled=True)
    multipliers = jnp.dot(back, choose.T, precision=lax.Precision.HIGHEST)
    return (multipliers, velocity)


def solution(mesh):
    in_specs = (
        P(None, "gx", "gy", None),
        P("gx", "gy", None),
        P(None, ("gx", "gy")),
        P(None, ("gx", "gy")),
        P(None, ("gx", "gy")),
        P(("gx", "gy"), None),
    )
    out_specs = (P(None, ("gx", "gy")), P(None, "gx", "gy", None))
    return jax.shard_map(shards, mesh=mesh, in_specs=in_specs, out_specs=out_specs, check_vma=False)
```

```python
import functools
import jax
import jax.numpy as jnp
from jax import lax
from jax.experimental import pallas as pl
from jax.experimental.pallas import tpu as pltpu
from jax.sharding import PartitionSpec as P

COMP = 3
NODES = 32
MULT = 81
ITERS = 4
CAP = 4
ROWS = 88
MESH = pl.DeviceIdType.MESH


def pieces(values):
    high = values.astype(jnp.bfloat16).astype(jnp.float32)
    return jnp.concatenate([high, values - high], axis=0).astype(jnp.bfloat16)


def uzawa_kernel(ngx, ngy, slots, strides, spans, force_ref, shift_ref, row_ref, col_ref,
                 place_ref, block_ref, gap_ref, mult_ref, out_ref, links, inv, grown, edge, face, sent, got, part,
                 line, total, far, face_sem, swap_sem, line_sem, far_sem):
    me_x, me_y = lax.axis_index("gx"), lax.axis_index("gy")
    nodes = row_ref.shape[1]
    quads = nodes // 128
    z_step, x_step = strides
    x_span, y_span = spans

    barrier = pltpu.get_barrier_semaphore()
    for o in range(1, ngx):
        pl.semaphore_signal(barrier, inc=1, device_id={"gx": lax.rem(me_x + o, ngx)}, device_id_type=MESH)
    for o in range(1, ngy):
        pl.semaphore_signal(barrier, inc=1, device_id={"gy": lax.rem(me_y + o, ngy)}, device_id_type=MESH)
    pl.semaphore_wait(barrier, ngx + ngy - 2)

    def exchange(source, slot):
        copies = []
        for side, (axis, me, count, step) in enumerate(
            (("gx", me_x, ngx, 1), ("gx", me_x, ngx, ngx - 1), ("gy", me_y, ngy, 1), ("gy", me_y, ngy, ngy - 1))
        ):
            copy = pltpu.make_async_remote_copy(
                src_ref=source, dst_ref=got.at[slot, side],
                send_sem=swap_sem.at[0, slot, side], recv_sem=swap_sem.at[1, slot, side],
                device_id={axis: lax.rem(me + step, count)}, device_id_type=MESH)
            copy.start()
            copies.append(copy)
        return copies

    _, cx, cy, cz = force_ref.shape
    columns = cx * cy
    spot = links.shape[0] - 1

    def start_faces(time):
        for c in range(COMP):
            edge[0, c] = grown[c, cx]
            edge[1, c] = grown[c, 1]
            edge[2, c] = grown[c, 1:cx + 1, cy - 1, :]
            edge[3, c] = grown[c, 1:cx + 1, 0, :]
        copies = []
        for side, (axis, me, count, step) in enumerate(
            (("gx", me_x, ngx, 1), ("gx", me_x, ngx, ngx - 1), ("gy", me_y, ngy, 1), ("gy", me_y, ngy, ngy - 1))
        ):
            copy = pltpu.make_async_remote_copy(
                src_ref=edge.at[side], dst_ref=face.at[time, side],
                send_sem=face_sem.at[0, time, side], recv_sem=face_sem.at[1, time, side],
                device_id={axis: lax.rem(me + step, count)}, device_id_type=MESH)
            copy.start()
            copies.append(copy)
        return copies

    def finish_smooth(copies, time):
        for copy in copies:
            copy.wait()
        for c in range(COMP):
            grown[c, 0] = jnp.where(me_x > 0, face[time, 0, c], 0.0)
            grown[c, cx + 1] = jnp.where(me_x < ngx - 1, face[time, 1, c], 0.0)
        y_at = lax.broadcasted_iota(jnp.int32, (cy, cz), 0)
        z_at = lax.broadcasted_iota(jnp.int32, (cy, cz), 1)

        @pl.loop(0, cx)
        def _(x):
            scale = inv[x]
            for c in range(COMP):
                mid = grown[c, x + 1]
                low = jnp.where(me_y > 0, face[time, 2, c, pl.ds(x, 1), :], 0.0)
                high = jnp.where(me_y < ngy - 1, face[time, 3, c, pl.ds(x, 1), :], 0.0)
                beside = grown[c, x] + grown[c, x + 2]
                beside = beside + jnp.where(y_at == 0, low, pltpu.roll(mid, 1, 0))
                beside = beside + jnp.where(y_at == cy - 1, high, pltpu.roll(mid, cy - 1, 0))
                beside = beside + jnp.where(z_at == 0, 0.0, pltpu.roll(mid, 1, 1))
                beside = beside + jnp.where(z_at == cz - 1, 0.0, pltpu.roll(mid, cz - 1, 1))
                out_ref[c, x] = mid + beside * scale

    def mark_spots():
        @pl.loop(0, columns // 128)
        def _(i):
            at = pl.multiple_of(i * 128, 128)
            here = lax.broadcasted_iota(jnp.int32, (128, nodes), 0) + at
            links[spot, pl.ds(at, 128), :] = jnp.where(here == place_ref[0:1, :], 1.0, 0.0).astype(jnp.bfloat16)

    def gather(field):
        high = field.astype(jnp.bfloat16).astype(jnp.float32)
        both = jnp.concatenate([high, field - high], axis=1).astype(jnp.bfloat16)
        picked = lax.dot_general(
            both, links[spot, 0:columns, :], (((0,), (0,)), ((), ())), preferred_element_type=jnp.float32)
        z_row = lax.broadcasted_iota(jnp.int32, (cz, nodes), 0) == place_ref[1:2, :]
        return jnp.sum(jnp.where(z_row, picked[:cz] + picked[cz:], 0.0), axis=0, keepdims=True)

    def scatter(values):
        high = values.astype(jnp.bfloat16).astype(jnp.float32)
        z_row = lax.broadcasted_iota(jnp.int32, (cz, nodes), 0) == place_ref[1:2, :]
        both = jnp.concatenate(
            [jnp.where(z_row, high, 0.0), jnp.where(z_row, values - high, 0.0)], axis=0).astype(jnp.bfloat16)
        summed = lax.dot_general(
            links[spot, 0:columns, :], both, (((1,), (1,)), ((), ())), preferred_element_type=jnp.float32)
        return (summed[:, :cz] + summed[:, cz:]).reshape(cx, cy, cz)

    inv[...] = 1.0 / (6.0 + shift_ref[...])
    for c in range(COMP):
        grown[c, 1:cx + 1] = force_ref[c] * inv[...]
    faces = start_faces(0)
    copies = exchange(row_ref, 0)
    tile = 128
    mark_spots()

    @pl.loop(0, nodes // tile)
    def _(i):
        at = pl.ds(pl.multiple_of(i * tile, tile), tile)
        gap = jnp.abs(row_ref[0:1, :] - col_ref[at, :])
        links[0, at, :] = jnp.where(gap == 0.0, 1.0, 0.0).astype(jnp.bfloat16)
        links[1, at, :] = jnp.where(
            (gap == 1.0) | (gap == z_step) | (gap == x_step), 1.0, 0.0).astype(jnp.bfloat16)

    finish_smooth(faces, 0)
    sent[...] = jnp.zeros_like(sent)
    part[...] = jnp.zeros_like(part)
    for c in range(COMP):
        sent[c:c + 1, :] = gather(out_ref[c].reshape(columns, cz))
    inverse = gather(inv[...].reshape(columns, cz))
    start = sent[...]

    for copy in copies:
        copy.wait()
    nowhere = jnp.float32(8.0 * (x_span + x_step))
    from_left = jnp.where(me_x > 0, x_step - x_span, nowhere).astype(jnp.float32)
    from_right = jnp.where(me_x < ngx - 1, x_span - x_step, nowhere).astype(jnp.float32)
    from_below = jnp.where(me_y > 0, z_step - y_span, nowhere).astype(jnp.float32)
    from_above = jnp.where(me_y < ngy - 1, y_span - z_step, nowhere).astype(jnp.float32)

    @pl.loop(0, nodes // tile)
    def _(i):
        at = pl.ds(pl.multiple_of(i * tile, tile), tile)
        own = col_ref[at, :]
        for side, offset in enumerate((from_left, from_right, from_below, from_above)):
            moved = got[0, side, 0:1, :] + offset
            links[2 + side, at, :] = jnp.where(moved == own, 1.0, 0.0).astype(jnp.bfloat16)

    def apply_link(kind, values):
        both = lax.dot_general(
            pieces(values), links[kind], (((1,), (1,)), ((), ())), preferred_element_type=jnp.float32)
        return both[0:8] + both[8:16]

    def apply_bt(multi, into):
        for c in range(COMP):
            for q in range(quads):
                into[c:c + 1, q * 128:(q + 1) * 128] = jnp.sum(
                    block_ref[c * quads + q] * multi, axis=0, keepdims=True)

    def apply_b(values):
        image = jnp.zeros((ROWS, 128), jnp.float32)
        for c in range(COMP):
            for q in range(quads):
                image = image + block_ref[c * quads + q] * values[c:c + 1, q * 128:(q + 1) * 128]
        shift = 64
        while shift >= slots:
            image = image + pltpu.roll(image, shift, 1)
            shift //= 2
        return image

    def all_sum(slot):
        for axis, me, count, source, room, sems in (
            ("gx", me_x, ngx, part, line, line_sem), ("gy", me_y, ngy, total, far, far_sem)):
            copies = []
            for o in range(1, count):
                copy = pltpu.make_async_remote_copy(
                    src_ref=source, dst_ref=room.at[slot, o],
                    send_sem=sems.at[0, slot, o], recv_sem=sems.at[1, slot, o],
                    device_id={axis: lax.rem(me + o, count)}, device_id_type=MESH)
                copy.start()
                copies.append(copy)
            summed = source[...]
            for o, copy in enumerate(copies):
                copy.wait()
                summed = summed + room[slot, o + 1]
            if axis == "gx":
                total[...] = summed
        return summed

    def step(iteration, state):
        multi, residual, direction = state
        apply_bt(direction, sent)
        scaled = sent[...] * inverse
        sent[...] = scaled
        copies = exchange(sent, iteration + 1)
        here = apply_link(0, scaled)
        beside = apply_link(1, scaled)
        for side, copy in enumerate(copies):
            copy.wait()
            beside = beside + apply_link(2 + side, got[iteration + 1, side])
        image = apply_b(here + beside * inverse)
        for row, (a, b) in enumerate(
            ((residual, residual), (direction, image), (residual, image), (image, image))):
            part[row:row + 1, :] = jnp.sum(a * b, axis=0, keepdims=True)
        sums = jnp.sum(all_sum(iteration), axis=1, keepdims=True)
        norm_now, bend, cross, square = sums[0:1], sums[1:2], sums[2:3], sums[3:4]
        step_size = norm_now / bend
        norm_next = norm_now - 2.0 * step_size * cross + step_size * step_size * square
        multi = multi + step_size * direction
        residual = residual - step_size * image
        direction = residual + norm_next / norm_now * direction
        return multi, residual, direction

    goal = apply_b(start) - gap_ref[...]
    multi, _, _ = lax.fori_loop(0, ITERS, step, (jnp.zeros_like(goal), goal, goal))
    mult_ref[...] = multi
    apply_bt(multi, sent)
    if spot < 6:
        mark_spots()
    for c in range(COMP):
        grown[c, 1:cx + 1] = (force_ref[c] - scatter(sent[c:c + 1, :])) * inv[...]
    finish_smooth(start_faces(1), 1)


def shards(body_force, shift_coef, coupling, node_cells, target_gap, new_owner):
    groups, rows_gy = lax.axis_size("gx"), lax.axis_size("gy")
    slots = groups * CAP
    pack = 128 // slots
    quads = NODES // pack
    nodes = NODES * slots
    owners = new_owner[:, 0]
    onehot = (owners[:, None] == jnp.arange(groups, dtype=jnp.int32)[None, :]).astype(jnp.int32)
    rank_in = jnp.sum((jnp.cumsum(onehot, axis=0) - 1) * onehot, axis=1)
    slot_of = owners * CAP + rank_in
    _, cx, cy, cz = body_force.shape
    cell_total = cx * cy * cz

    held = jnp.concatenate([coupling, node_cells.astype(jnp.float32), target_gap], axis=0)
    choose = (slot_of[:, None] == jnp.arange(slots, dtype=jnp.int32)[None, :]).astype(jnp.float32)
    held = jnp.dot(held, choose, precision=lax.Precision.HIGHEST)
    moved = lax.all_to_all(held, "gx", split_axis=1, concat_axis=1, tiled=True)
    block_rows = COMP * NODES * MULT
    blocks = moved[:block_rows].reshape(COMP * quads, pack, MULT, slots)
    blocks = jnp.pad(blocks.transpose(0, 2, 1, 3).reshape(COMP * quads, MULT, 128), ((0, 0), (0, ROWS - MULT), (0, 0)))
    cell_int = jnp.round(moved[block_rows:block_rows + NODES]).astype(jnp.int32).reshape(nodes)
    gap = moved[block_rows + NODES:]

    z_step = cz + 2
    x_step = z_step * (3 * cy + 4)
    ids = (cell_int // (cy * cz) * x_step + cell_int // cz % cy * z_step + cell_int % cz).astype(jnp.float32)
    gap = jnp.tile(jnp.pad(gap, ((0, ROWS - MULT), (0, 0))), (1, pack))
    place = jnp.pad(jnp.stack([cell_int // cz, cell_int % cz]), ((0, 6), (0, 0)))

    vmem = pl.BlockSpec(memory_space=pltpu.VMEM)
    multi, velocity = pl.pallas_call(
        functools.partial(
            uzawa_kernel, groups, rows_gy, slots, (float(z_step), float(x_step)),
            (float(cx * x_step), float(cy * z_step))),
        out_shape=(
            jax.ShapeDtypeStruct((ROWS, 128), jnp.float32),
            jax.ShapeDtypeStruct(body_force.shape, jnp.float32),
        ),
        in_specs=[vmem] * 7,
        out_specs=(vmem, vmem),
        scratch_shapes=[
            pltpu.VMEM((7 if nodes <= 1024 else 6, nodes, nodes), jnp.bfloat16),
            pltpu.VMEM((cx, cy, cz), jnp.float32),
            pltpu.VMEM((COMP, cx + 2, cy, cz), jnp.float32),
            pltpu.VMEM((4, COMP, cy, cz), jnp.float32),
            pltpu.VMEM((2, 4, COMP, cy, cz), jnp.float32),
            pltpu.VMEM((8, nodes), jnp.float32),
            pltpu.VMEM((ITERS + 1, 4, 8, nodes), jnp.float32),
            pltpu.VMEM((8, 128), jnp.float32),
            pltpu.VMEM((ITERS, groups, 8, 128), jnp.float32),
            pltpu.VMEM((8, 128), jnp.float32),
            pltpu.VMEM((ITERS, rows_gy, 8, 128), jnp.float32),
            pltpu.SemaphoreType.DMA((2, 2, 4)),
            pltpu.SemaphoreType.DMA((2, ITERS + 1, 4)),
            pltpu.SemaphoreType.DMA((2, ITERS, groups)),
            pltpu.SemaphoreType.DMA((2, ITERS, rows_gy)),
        ],
        compiler_params=pltpu.CompilerParams(
            collective_id=0, has_side_effects=True,
            vmem_limit_bytes=(46 << 20) if nodes <= 1024 else (63 << 20)),
    )(
        body_force, shift_coef, jnp.broadcast_to(ids[None], (8, nodes)), ids[:, None], place, blocks, gap,
    )

    back = lax.all_to_all(multi[:MULT, :slots], "gx", split_axis=1, concat_axis=1, tiled=True)
    multipliers = jnp.dot(back, choose.T, precision=lax.Precision.HIGHEST)
    return (multipliers, velocity)


def solution(mesh):
    in_specs = (
        P(None, "gx", "gy", None),
        P("gx", "gy", None),
        P(None, ("gx", "gy")),
        P(None, ("gx", "gy")),
        P(None, ("gx", "gy")),
        P(("gx", "gy"), None),
    )
    out_specs = (P(None, ("gx", "gy")), P(None, "gx", "gy", None))
    return jax.shard_map(shards, mesh=mesh, in_specs=in_specs, out_specs=out_specs, check_vma=False)
```

```python
import functools
import jax
import jax.numpy as jnp
from jax import lax
from jax.experimental import pallas as pl
from jax.experimental.pallas import tpu as pltpu
from jax.sharding import PartitionSpec as P

COMP = 3
NODES = 32
MULT = 81
ITERS = 4
CAP = 4
ROWS = 88
MESH = pl.DeviceIdType.MESH


def pieces(values):
    high = values.astype(jnp.bfloat16).astype(jnp.float32)
    return jnp.concatenate([high, values - high], axis=0).astype(jnp.bfloat16)


def uzawa_kernel(ngx, ngy, slots, strides, spans, force_ref, shift_ref, row_ref, col_ref,
                 place_ref, block_ref, gap_ref, mult_ref, out_ref, links, inv, grown, edge, face, sent, got, part,
                 line, total, far, face_sem, swap_sem, line_sem, far_sem):
    me_x, me_y = lax.axis_index("gx"), lax.axis_index("gy")
    nodes = row_ref.shape[1]
    quads = nodes // 128
    z_step, x_step = strides
    x_span, y_span = spans

    barrier = pltpu.get_barrier_semaphore()
    for o in range(1, ngx):
        pl.semaphore_signal(barrier, inc=1, device_id={"gx": lax.rem(me_x + o, ngx)}, device_id_type=MESH)
    for o in range(1, ngy):
        pl.semaphore_signal(barrier, inc=1, device_id={"gy": lax.rem(me_y + o, ngy)}, device_id_type=MESH)
    pl.semaphore_wait(barrier, ngx + ngy - 2)

    def exchange(source, slot):
        copies = []
        for side, (axis, me, count, step) in enumerate(
            (("gx", me_x, ngx, 1), ("gx", me_x, ngx, ngx - 1), ("gy", me_y, ngy, 1), ("gy", me_y, ngy, ngy - 1))
        ):
            copy = pltpu.make_async_remote_copy(
                src_ref=source, dst_ref=got.at[slot, side],
                send_sem=swap_sem.at[0, slot, side], recv_sem=swap_sem.at[1, slot, side],
                device_id={axis: lax.rem(me + step, count)}, device_id_type=MESH)
            copy.start()
            copies.append(copy)
        return copies

    _, cx, cy, cz = force_ref.shape
    columns = cx * cy
    spot = links.shape[0] - 1

    def start_faces(time):
        for c in range(COMP):
            edge[0, c] = grown[c, cx]
            edge[1, c] = grown[c, 1]
            edge[2, c] = grown[c, 1:cx + 1, cy - 1, :]
            edge[3, c] = grown[c, 1:cx + 1, 0, :]
        copies = []
        for side, (axis, me, count, step) in enumerate(
            (("gx", me_x, ngx, 1), ("gx", me_x, ngx, ngx - 1), ("gy", me_y, ngy, 1), ("gy", me_y, ngy, ngy - 1))
        ):
            copy = pltpu.make_async_remote_copy(
                src_ref=edge.at[side], dst_ref=face.at[time, side],
                send_sem=face_sem.at[0, time, side], recv_sem=face_sem.at[1, time, side],
                device_id={axis: lax.rem(me + step, count)}, device_id_type=MESH)
            copy.start()
            copies.append(copy)
        return copies

    def finish_smooth(copies, time):
        for copy in copies:
            copy.wait()
        for c in range(COMP):
            grown[c, 0] = jnp.where(me_x > 0, face[time, 0, c], 0.0)
            grown[c, cx + 1] = jnp.where(me_x < ngx - 1, face[time, 1, c], 0.0)
        y_at = lax.broadcasted_iota(jnp.int32, (cy, cz), 0)
        z_at = lax.broadcasted_iota(jnp.int32, (cy, cz), 1)

        @pl.loop(0, cx)
        def _(x):
            scale = inv[x]
            for c in range(COMP):
                mid = grown[c, x + 1]
                low = jnp.where(me_y > 0, face[time, 2, c, pl.ds(x, 1), :], 0.0)
                high = jnp.where(me_y < ngy - 1, face[time, 3, c, pl.ds(x, 1), :], 0.0)
                beside = grown[c, x] + grown[c, x + 2]
                beside = beside + jnp.where(y_at == 0, low, pltpu.roll(mid, 1, 0))
                beside = beside + jnp.where(y_at == cy - 1, high, pltpu.roll(mid, cy - 1, 0))
                beside = beside + jnp.where(z_at == 0, 0.0, pltpu.roll(mid, 1, 1))
                beside = beside + jnp.where(z_at == cz - 1, 0.0, pltpu.roll(mid, cz - 1, 1))
                out_ref[c, x] = mid + beside * scale

    def mark_spots():
        @pl.loop(0, columns // 128)
        def _(i):
            at = pl.multiple_of(i * 128, 128)
            here = lax.broadcasted_iota(jnp.int32, (128, nodes), 0) + at
            links[spot, pl.ds(at, 128), :] = jnp.where(here == place_ref[0:1, :], 1.0, 0.0).astype(jnp.bfloat16)

    def gather(field):
        high = field.astype(jnp.bfloat16).astype(jnp.float32)
        both = jnp.concatenate([high, field - high], axis=1).astype(jnp.bfloat16)
        picked = lax.dot_general(
            both, links[spot, 0:columns, :], (((0,), (0,)), ((), ())), preferred_element_type=jnp.float32)
        z_row = lax.broadcasted_iota(jnp.int32, (cz, nodes), 0) == place_ref[1:2, :]
        return jnp.sum(jnp.where(z_row, picked[:cz] + picked[cz:], 0.0), axis=0, keepdims=True)

    def scatter(values):
        high = values.astype(jnp.bfloat16).astype(jnp.float32)
        z_row = lax.broadcasted_iota(jnp.int32, (cz, nodes), 0) == place_ref[1:2, :]
        both = jnp.concatenate(
            [jnp.where(z_row, high, 0.0), jnp.where(z_row, values - high, 0.0)], axis=0).astype(jnp.bfloat16)
        summed = lax.dot_general(
            links[spot, 0:columns, :], both, (((1,), (1,)), ((), ())), preferred_element_type=jnp.float32)
        return (summed[:, :cz] + summed[:, cz:]).reshape(cx, cy, cz)

    inv[...] = 1.0 / (6.0 + shift_ref[...])
    for c in range(COMP):
        grown[c, 1:cx + 1] = force_ref[c] * inv[...]
    faces = start_faces(0)
    copies = exchange(row_ref, 0)
    tile = 128
    mark_spots()

    @pl.loop(0, nodes // tile)
    def _(i):
        at = pl.ds(pl.multiple_of(i * tile, tile), tile)
        gap = jnp.abs(row_ref[0:1, :] - col_ref[at, :])
        links[0, at, :] = jnp.where(gap == 0.0, 1.0, 0.0).astype(jnp.bfloat16)
        links[1, at, :] = jnp.where(
            (gap == 1.0) | (gap == z_step) | (gap == x_step), 1.0, 0.0).astype(jnp.bfloat16)

    finish_smooth(faces, 0)
    sent[...] = jnp.zeros_like(sent)
    part[...] = jnp.zeros_like(part)
    for c in range(COMP):
        sent[c:c + 1, :] = gather(out_ref[c].reshape(columns, cz))
    inverse = gather(inv[...].reshape(columns, cz))
    start = sent[...]

    for copy in copies:
        copy.wait()
    nowhere = jnp.float32(8.0 * (x_span + x_step))
    from_left = jnp.where(me_x > 0, x_step - x_span, nowhere).astype(jnp.float32)
    from_right = jnp.where(me_x < ngx - 1, x_span - x_step, nowhere).astype(jnp.float32)
    from_below = jnp.where(me_y > 0, z_step - y_span, nowhere).astype(jnp.float32)
    from_above = jnp.where(me_y < ngy - 1, y_span - z_step, nowhere).astype(jnp.float32)

    @pl.loop(0, nodes // tile)
    def _(i):
        at = pl.ds(pl.multiple_of(i * tile, tile), tile)
        own = col_ref[at, :]
        for side, offset in enumerate((from_left, from_right, from_below, from_above)):
            moved = got[0, side, 0:1, :] + offset
            links[2 + side, at, :] = jnp.where(moved == own, 1.0, 0.0).astype(jnp.bfloat16)

    def apply_link(kind, values):
        both = lax.dot_general(
            pieces(values), links[kind], (((1,), (1,)), ((), ())), preferred_element_type=jnp.float32)
        return both[0:8] + both[8:16]

    def apply_bt(multi, into):
        for c in range(COMP):
            for q in range(quads):
                into[c:c + 1, q * 128:(q + 1) * 128] = jnp.sum(
                    block_ref[c * quads + q] * multi, axis=0, keepdims=True)

    def apply_b(values):
        image = jnp.zeros((ROWS, 128), jnp.float32)
        for c in range(COMP):
            for q in range(quads):
                image = image + block_ref[c * quads + q] * values[c:c + 1, q * 128:(q + 1) * 128]
        shift = 64
        while shift >= slots:
            image = image + pltpu.roll(image, shift, 1)
            shift //= 2
        return image

    def send_part(slot, stage):
        axis, me, count, source, room, sems = (
            ("gx", me_x, ngx, part, line, line_sem), ("gy", me_y, ngy, total, far, far_sem))[stage]
        copies = []
        for o in range(1, count):
            copy = pltpu.make_async_remote_copy(
                src_ref=source, dst_ref=room.at[slot, o],
                send_sem=sems.at[0, slot, o], recv_sem=sems.at[1, slot, o],
                device_id={axis: lax.rem(me + o, count)}, device_id_type=MESH)
            copy.start()
            copies.append(copy)
        return copies

    def add_parts(copies, slot, stage):
        source, room = ((part, line), (total, far))[stage]
        summed = source[...]
        for o, copy in enumerate(copies):
            copy.wait()
            summed = summed + room[slot, o + 1]
        return summed

    def start_image(field, slot):
        apply_bt(field, sent)
        scaled = sent[...] * inverse
        sent[...] = scaled
        return scaled, exchange(sent, slot)

    def local_image(scaled):
        return apply_link(0, scaled), apply_link(1, scaled)

    def finish_image(copies, slot, here, beside):
        for side, copy in enumerate(copies):
            copy.wait()
            beside = beside + apply_link(2 + side, got[slot, side])
        return apply_b(here + beside * inverse)

    def form_part(residual, direction, image):
        for row, (a, b) in enumerate(
            ((residual, residual), (direction, image), (residual, image), (image, image))):
            part[row:row + 1, :] = jnp.sum(a * b, axis=0, keepdims=True)

    def coefficients(tile_sum):
        sums = jnp.sum(tile_sum, axis=1, keepdims=True)
        norm_now, bend, cross, square = sums[0:1], sums[1:2], sums[2:3], sums[3:4]
        step_size = norm_now / bend
        norm_next = norm_now - 2.0 * step_size * cross + step_size * step_size * square
        return step_size, norm_next / norm_now

    def step(iteration, state):
        multi, residual, direction, image, reach = state
        form_part(residual, direction, image)
        parts = send_part(iteration, 0)
        scaled, copies = start_image(image, iteration + 2)
        here, beside = local_image(scaled)
        total[...] = add_parts(parts, iteration, 0)
        parts = send_part(iteration, 1)
        second = finish_image(copies, iteration + 2, here, beside)
        step_size, ratio = coefficients(add_parts(parts, iteration, 1))
        multi = multi + step_size * direction
        residual = residual - step_size * image
        reach = reach - step_size * second
        direction = residual + ratio * direction
        image = reach + ratio * image
        return multi, residual, direction, image, reach

    goal = apply_b(start) - gap_ref[...]
    scaled, copies = start_image(goal, 1)
    here, beside = local_image(scaled)
    image = finish_image(copies, 1, here, beside)
    multi, residual, direction, image, _ = lax.fori_loop(
        0, ITERS - 1, step, (jnp.zeros_like(goal), goal, goal, image, image))
    form_part(residual, direction, image)
    total[...] = add_parts(send_part(ITERS - 1, 0), ITERS - 1, 0)
    step_size, _ = coefficients(add_parts(send_part(ITERS - 1, 1), ITERS - 1, 1))
    multi = multi + step_size * direction
    mult_ref[...] = multi
    apply_bt(multi, sent)
    if spot < 6:
        mark_spots()
    for c in range(COMP):
        grown[c, 1:cx + 1] = (force_ref[c] - scatter(sent[c:c + 1, :])) * inv[...]
    finish_smooth(start_faces(1), 1)


def shards(body_force, shift_coef, coupling, node_cells, target_gap, new_owner):
    groups, rows_gy = lax.axis_size("gx"), lax.axis_size("gy")
    slots = groups * CAP
    pack = 128 // slots
    quads = NODES // pack
    nodes = NODES * slots
    owners = new_owner[:, 0]
    onehot = (owners[:, None] == jnp.arange(groups, dtype=jnp.int32)[None, :]).astype(jnp.int32)
    rank_in = jnp.sum((jnp.cumsum(onehot, axis=0) - 1) * onehot, axis=1)
    slot_of = owners * CAP + rank_in
    _, cx, cy, cz = body_force.shape
    cell_total = cx * cy * cz

    held = jnp.concatenate([coupling, node_cells.astype(jnp.float32), target_gap], axis=0)
    choose = (slot_of[:, None] == jnp.arange(slots, dtype=jnp.int32)[None, :]).astype(jnp.float32)
    held = jnp.dot(held, choose, precision=lax.Precision.HIGHEST)
    moved = lax.all_to_all(held, "gx", split_axis=1, concat_axis=1, tiled=True)
    block_rows = COMP * NODES * MULT
    blocks = moved[:block_rows].reshape(COMP * quads, pack, MULT, slots)
    blocks = jnp.pad(blocks.transpose(0, 2, 1, 3).reshape(COMP * quads, MULT, 128), ((0, 0), (0, ROWS - MULT), (0, 0)))
    cell_int = jnp.round(moved[block_rows:block_rows + NODES]).astype(jnp.int32).reshape(nodes)
    gap = moved[block_rows + NODES:]

    z_step = cz + 2
    x_step = z_step * (3 * cy + 4)
    ids = (cell_int // (cy * cz) * x_step + cell_int // cz % cy * z_step + cell_int % cz).astype(jnp.float32)
    gap = jnp.tile(jnp.pad(gap, ((0, ROWS - MULT), (0, 0))), (1, pack))
    place = jnp.pad(jnp.stack([cell_int // cz, cell_int % cz]), ((0, 6), (0, 0)))

    vmem = pl.BlockSpec(memory_space=pltpu.VMEM)
    multi, velocity = pl.pallas_call(
        functools.partial(
            uzawa_kernel, groups, rows_gy, slots, (float(z_step), float(x_step)),
            (float(cx * x_step), float(cy * z_step))),
        out_shape=(
            jax.ShapeDtypeStruct((ROWS, 128), jnp.float32),
            jax.ShapeDtypeStruct(body_force.shape, jnp.float32),
        ),
        in_specs=[vmem] * 7,
        out_specs=(vmem, vmem),
        scratch_shapes=[
            pltpu.VMEM((7 if nodes <= 1024 else 6, nodes, nodes), jnp.bfloat16),
            pltpu.VMEM((cx, cy, cz), jnp.float32),
            pltpu.VMEM((COMP, cx + 2, cy, cz), jnp.float32),
            pltpu.VMEM((4, COMP, cy, cz), jnp.float32),
            pltpu.VMEM((2, 4, COMP, cy, cz), jnp.float32),
            pltpu.VMEM((8, nodes), jnp.float32),
            pltpu.VMEM((ITERS + 1, 4, 8, nodes), jnp.float32),
            pltpu.VMEM((8, 128), jnp.float32),
            pltpu.VMEM((ITERS, groups, 8, 128), jnp.float32),
            pltpu.VMEM((8, 128), jnp.float32),
            pltpu.VMEM((ITERS, rows_gy, 8, 128), jnp.float32),
            pltpu.SemaphoreType.DMA((2, 2, 4)),
            pltpu.SemaphoreType.DMA((2, ITERS + 1, 4)),
            pltpu.SemaphoreType.DMA((2, ITERS, groups)),
            pltpu.SemaphoreType.DMA((2, ITERS, rows_gy)),
        ],
        compiler_params=pltpu.CompilerParams(
            collective_id=0, has_side_effects=True,
            vmem_limit_bytes=(46 << 20) if nodes <= 1024 else (63 << 20)),
    )(
        body_force, shift_coef, jnp.broadcast_to(ids[None], (8, nodes)), ids[:, None], place, blocks, gap,
    )

    back = lax.all_to_all(multi[:MULT, :slots], "gx", split_axis=1, concat_axis=1, tiled=True)
    multipliers = jnp.dot(back, choose.T, precision=lax.Precision.HIGHEST)
    return (multipliers, velocity)


def solution(mesh):
    in_specs = (
        P(None, "gx", "gy", None),
        P("gx", "gy", None),
        P(None, ("gx", "gy")),
        P(None, ("gx", "gy")),
        P(None, ("gx", "gy")),
        P(("gx", "gy"), None),
    )
    out_specs = (P(None, ("gx", "gy")), P(None, "gx", "gy", None))
    return jax.shard_map(shards, mesh=mesh, in_specs=in_specs, out_specs=out_specs, check_vma=False)
```

```python
import functools
import jax
import jax.numpy as jnp
from jax import lax
from jax.experimental import pallas as pl
from jax.experimental.pallas import tpu as pltpu
from jax.sharding import PartitionSpec as P

COMP = 3
NODES = 32
MULT = 81
ITERS = 4
CAP = 4
ROWS = 88
MESH = pl.DeviceIdType.MESH


def pieces(values):
    high = values.astype(jnp.bfloat16).astype(jnp.float32)
    return jnp.concatenate([high, values - high], axis=0).astype(jnp.bfloat16)


def uzawa_kernel(ngx, ngy, slots, strides, spans, force_ref, shift_ref, row_ref, col_ref,
                 place_ref, block_ref, gap_ref, mult_ref, out_ref, links, inv, grown, edge, face, sent, got, part,
                 line, total, far, own, home, face_sem, home_sem, swap_sem, line_sem, far_sem):
    me_x, me_y = lax.axis_index("gx"), lax.axis_index("gy")
    nodes = row_ref.shape[1]
    quads = nodes // 128
    z_step, x_step = strides
    x_span, y_span = spans

    barrier = pltpu.get_barrier_semaphore()
    for o in range(1, ngx):
        pl.semaphore_signal(barrier, inc=1, device_id={"gx": lax.rem(me_x + o, ngx)}, device_id_type=MESH)
    for o in range(1, ngy):
        pl.semaphore_signal(barrier, inc=1, device_id={"gy": lax.rem(me_y + o, ngy)}, device_id_type=MESH)
    pl.semaphore_wait(barrier, ngx + ngy - 2)

    def exchange(source, slot):
        copies = []
        for side, (axis, me, count, step) in enumerate(
            (("gx", me_x, ngx, 1), ("gx", me_x, ngx, ngx - 1), ("gy", me_y, ngy, 1), ("gy", me_y, ngy, ngy - 1))
        ):
            copy = pltpu.make_async_remote_copy(
                src_ref=source, dst_ref=got.at[slot, side],
                send_sem=swap_sem.at[0, slot, side], recv_sem=swap_sem.at[1, slot, side],
                device_id={axis: lax.rem(me + step, count)}, device_id_type=MESH)
            copy.start()
            copies.append(copy)
        return copies

    _, cx, cy, cz = force_ref.shape
    columns = cx * cy
    spot = links.shape[0] - 1

    def start_faces(time):
        for c in range(COMP):
            edge[0, c] = grown[c, cx]
            edge[1, c] = grown[c, 1]
            edge[2, c] = grown[c, 1:cx + 1, cy - 1, :]
            edge[3, c] = grown[c, 1:cx + 1, 0, :]
        copies = []
        for side, (axis, me, count, step) in enumerate(
            (("gx", me_x, ngx, 1), ("gx", me_x, ngx, ngx - 1), ("gy", me_y, ngy, 1), ("gy", me_y, ngy, ngy - 1))
        ):
            copy = pltpu.make_async_remote_copy(
                src_ref=edge.at[side], dst_ref=face.at[time, side],
                send_sem=face_sem.at[0, time, side], recv_sem=face_sem.at[1, time, side],
                device_id={axis: lax.rem(me + step, count)}, device_id_type=MESH)
            copy.start()
            copies.append(copy)
        return copies

    def finish_smooth(copies, time):
        for copy in copies:
            copy.wait()
        for c in range(COMP):
            grown[c, 0] = jnp.where(me_x > 0, face[time, 0, c], 0.0)
            grown[c, cx + 1] = jnp.where(me_x < ngx - 1, face[time, 1, c], 0.0)
        y_at = lax.broadcasted_iota(jnp.int32, (cy, cz), 0)
        z_at = lax.broadcasted_iota(jnp.int32, (cy, cz), 1)

        @pl.loop(0, cx)
        def _(x):
            scale = inv[x]
            for c in range(COMP):
                mid = grown[c, x + 1]
                low = jnp.where(me_y > 0, face[time, 2, c, pl.ds(x, 1), :], 0.0)
                high = jnp.where(me_y < ngy - 1, face[time, 3, c, pl.ds(x, 1), :], 0.0)
                beside = grown[c, x] + grown[c, x + 2]
                beside = beside + jnp.where(y_at == 0, low, pltpu.roll(mid, 1, 0))
                beside = beside + jnp.where(y_at == cy - 1, high, pltpu.roll(mid, cy - 1, 0))
                beside = beside + jnp.where(z_at == 0, 0.0, pltpu.roll(mid, 1, 1))
                beside = beside + jnp.where(z_at == cz - 1, 0.0, pltpu.roll(mid, cz - 1, 1))
                out_ref[c, x] = mid + beside * scale

    def mark_spots():
        @pl.loop(0, columns // 128)
        def _(i):
            at = pl.multiple_of(i * 128, 128)
            here = lax.broadcasted_iota(jnp.int32, (128, nodes), 0) + at
            links[spot, pl.ds(at, 128), :] = jnp.where(here == place_ref[0:1, :], 1.0, 0.0).astype(jnp.bfloat16)

    def gather(field):
        high = field.astype(jnp.bfloat16).astype(jnp.float32)
        both = jnp.concatenate([high, field - high], axis=1).astype(jnp.bfloat16)
        picked = lax.dot_general(
            both, links[spot, 0:columns, :], (((0,), (0,)), ((), ())), preferred_element_type=jnp.float32)
        z_row = lax.broadcasted_iota(jnp.int32, (cz, nodes), 0) == place_ref[1:2, :]
        return jnp.sum(jnp.where(z_row, picked[:cz] + picked[cz:], 0.0), axis=0, keepdims=True)

    def scatter(values):
        high = values.astype(jnp.bfloat16).astype(jnp.float32)
        z_row = lax.broadcasted_iota(jnp.int32, (cz, nodes), 0) == place_ref[1:2, :]
        both = jnp.concatenate(
            [jnp.where(z_row, high, 0.0), jnp.where(z_row, values - high, 0.0)], axis=0).astype(jnp.bfloat16)
        summed = lax.dot_general(
            links[spot, 0:columns, :], both, (((1,), (1,)), ((), ())), preferred_element_type=jnp.float32)
        return (summed[:, :cz] + summed[:, cz:]).reshape(cx, cy, cz)

    inv[...] = 1.0 / (6.0 + shift_ref[...])
    for c in range(COMP):
        grown[c, 1:cx + 1] = force_ref[c] * inv[...]
    faces = start_faces(0)
    copies = exchange(row_ref, 0)
    tile = 128
    mark_spots()

    @pl.loop(0, nodes // tile)
    def _(i):
        at = pl.ds(pl.multiple_of(i * tile, tile), tile)
        gap = jnp.abs(row_ref[0:1, :] - col_ref[at, :])
        links[0, at, :] = jnp.where(gap == 0.0, 1.0, 0.0).astype(jnp.bfloat16)
        links[1, at, :] = jnp.where(
            (gap == 1.0) | (gap == z_step) | (gap == x_step), 1.0, 0.0).astype(jnp.bfloat16)

    finish_smooth(faces, 0)
    sent[...] = jnp.zeros_like(sent)
    part[...] = jnp.zeros_like(part)
    for c in range(COMP):
        sent[c:c + 1, :] = gather(out_ref[c].reshape(columns, cz))
    inverse = gather(inv[...].reshape(columns, cz))
    start = sent[...]

    for copy in copies:
        copy.wait()
    nowhere = jnp.float32(8.0 * (x_span + x_step))
    from_left = jnp.where(me_x > 0, x_step - x_span, nowhere).astype(jnp.float32)
    from_right = jnp.where(me_x < ngx - 1, x_span - x_step, nowhere).astype(jnp.float32)
    from_below = jnp.where(me_y > 0, z_step - y_span, nowhere).astype(jnp.float32)
    from_above = jnp.where(me_y < ngy - 1, y_span - z_step, nowhere).astype(jnp.float32)

    @pl.loop(0, nodes // tile)
    def _(i):
        at = pl.ds(pl.multiple_of(i * tile, tile), tile)
        own = col_ref[at, :]
        for side, offset in enumerate((from_left, from_right, from_below, from_above)):
            moved = got[0, side, 0:1, :] + offset
            links[2 + side, at, :] = jnp.where(moved == own, 1.0, 0.0).astype(jnp.bfloat16)

    def apply_link(kind, values):
        both = lax.dot_general(
            pieces(values), links[kind], (((1,), (1,)), ((), ())), preferred_element_type=jnp.float32)
        return both[0:8] + both[8:16]

    def apply_bt(multi, into):
        for c in range(COMP):
            for q in range(quads):
                into[c:c + 1, q * 128:(q + 1) * 128] = jnp.sum(
                    block_ref[c * quads + q] * multi, axis=0, keepdims=True)

    def apply_b(values):
        image = jnp.zeros((ROWS, 128), jnp.float32)
        for c in range(COMP):
            for q in range(quads):
                image = image + block_ref[c * quads + q] * values[c:c + 1, q * 128:(q + 1) * 128]
        shift = 64
        while shift >= slots:
            image = image + pltpu.roll(image, shift, 1)
            shift //= 2
        return image

    def send_part(slot, stage):
        axis, me, count, source, room, sems = (
            ("gx", me_x, ngx, part, line, line_sem), ("gy", me_y, ngy, total, far, far_sem))[stage]
        copies = []
        for o in range(1, count):
            copy = pltpu.make_async_remote_copy(
                src_ref=source, dst_ref=room.at[slot, o],
                send_sem=sems.at[0, slot, o], recv_sem=sems.at[1, slot, o],
                device_id={axis: lax.rem(me + o, count)}, device_id_type=MESH)
            copy.start()
            copies.append(copy)
        return copies

    def add_parts(copies, slot, stage):
        source, room = ((part, line), (total, far))[stage]
        summed = source[...]
        for o, copy in enumerate(copies):
            copy.wait()
            summed = summed + room[slot, o + 1]
        return summed

    def start_image(field, slot):
        apply_bt(field, sent)
        scaled = sent[...] * inverse
        sent[...] = scaled
        return scaled, exchange(sent, slot)

    def local_image(scaled):
        return apply_link(0, scaled), apply_link(1, scaled)

    def finish_image(copies, slot, here, beside):
        for side, copy in enumerate(copies):
            copy.wait()
            beside = beside + apply_link(2 + side, got[slot, side])
        return apply_b(here + beside * inverse)

    def form_part(residual, direction, image):
        for row, (a, b) in enumerate(
            ((residual, residual), (direction, image), (residual, image), (image, image))):
            part[row:row + 1, :] = jnp.sum(a * b, axis=0, keepdims=True)

    def coefficients(tile_sum):
        sums = jnp.sum(tile_sum, axis=1, keepdims=True)
        norm_now, bend, cross, square = sums[0:1], sums[1:2], sums[2:3], sums[3:4]
        step_size = norm_now / bend
        norm_next = norm_now - 2.0 * step_size * cross + step_size * step_size * square
        return step_size, norm_next / norm_now

    def step(iteration, state):
        multi, residual, direction, image, reach = state
        form_part(residual, direction, image)
        parts = send_part(iteration, 0)
        scaled, copies = start_image(image, iteration + 2)
        here, beside = local_image(scaled)
        total[...] = add_parts(parts, iteration, 0)
        parts = send_part(iteration, 1)
        second = finish_image(copies, iteration + 2, here, beside)
        step_size, ratio = coefficients(add_parts(parts, iteration, 1))
        multi = multi + step_size * direction
        residual = residual - step_size * image
        reach = reach - step_size * second
        direction = residual + ratio * direction
        image = reach + ratio * image
        return multi, residual, direction, image, reach

    goal = apply_b(start) - gap_ref[...]
    scaled, copies = start_image(goal, 1)
    here, beside = local_image(scaled)
    image = finish_image(copies, 1, here, beside)
    multi, residual, direction, image, _ = lax.fori_loop(
        0, ITERS - 1, step, (jnp.zeros_like(goal), goal, goal, image, image))
    form_part(residual, direction, image)
    total[...] = add_parts(send_part(ITERS - 1, 0), ITERS - 1, 0)
    step_size, _ = coefficients(add_parts(send_part(ITERS - 1, 1), ITERS - 1, 1))
    multi = multi + step_size * direction
    own[...] = multi
    returns = []
    for o in range(1, ngx):
        copy = pltpu.make_async_remote_copy(
            src_ref=own, dst_ref=home.at[o], send_sem=home_sem.at[0, o], recv_sem=home_sem.at[1, o],
            device_id={"gx": lax.rem(me_x + o, ngx)}, device_id_type=MESH)
        copy.start()
        returns.append(copy)
    apply_bt(multi, sent)
    if spot < 6:
        mark_spots()
    for c in range(COMP):
        grown[c, 1:cx + 1] = (force_ref[c] - scatter(sent[c:c + 1, :])) * inv[...]
    finish_smooth(start_faces(1), 1)
    lane = lax.broadcasted_iota(jnp.int32, (ROWS, 128), 1) // CAP
    collected = jnp.zeros((ROWS, 128), jnp.float32)
    for o in range(ngx):
        if o:
            returns[o - 1].wait()
        tile_of = home[o] if o else own[...]
        turned = pltpu.roll(tile_of, lax.rem(o * CAP + 128 - me_x * CAP, 128), 1)
        collected = jnp.where(lane == o, turned, collected)
    mult_ref[...] = collected


def shards(body_force, shift_coef, coupling, node_cells, target_gap, new_owner):
    groups, rows_gy = lax.axis_size("gx"), lax.axis_size("gy")
    slots = groups * CAP
    pack = 128 // slots
    quads = NODES // pack
    nodes = NODES * slots
    owners = new_owner[:, 0]
    onehot = (owners[:, None] == jnp.arange(groups, dtype=jnp.int32)[None, :]).astype(jnp.int32)
    rank_in = jnp.sum((jnp.cumsum(onehot, axis=0) - 1) * onehot, axis=1)
    slot_of = owners * CAP + rank_in
    _, cx, cy, cz = body_force.shape
    cell_total = cx * cy * cz

    held = jnp.concatenate([coupling, node_cells.astype(jnp.float32), target_gap], axis=0)
    choose = (slot_of[:, None] == jnp.arange(slots, dtype=jnp.int32)[None, :]).astype(jnp.float32)
    held = jnp.dot(held, choose, precision=lax.Precision.HIGHEST)
    moved = lax.all_to_all(held, "gx", split_axis=1, concat_axis=1, tiled=True)
    block_rows = COMP * NODES * MULT
    blocks = moved[:block_rows].reshape(COMP * quads, pack, MULT, slots)
    blocks = jnp.pad(blocks.transpose(0, 2, 1, 3).reshape(COMP * quads, MULT, 128), ((0, 0), (0, ROWS - MULT), (0, 0)))
    cell_int = jnp.round(moved[block_rows:block_rows + NODES]).astype(jnp.int32).reshape(nodes)
    gap = moved[block_rows + NODES:]

    z_step = cz + 2
    x_step = z_step * (3 * cy + 4)
    ids = (cell_int // (cy * cz) * x_step + cell_int // cz % cy * z_step + cell_int % cz).astype(jnp.float32)
    gap = jnp.tile(jnp.pad(gap, ((0, ROWS - MULT), (0, 0))), (1, pack))
    place = jnp.pad(jnp.stack([cell_int // cz, cell_int % cz]), ((0, 6), (0, 0)))

    vmem = pl.BlockSpec(memory_space=pltpu.VMEM)
    multi, velocity = pl.pallas_call(
        functools.partial(
            uzawa_kernel, groups, rows_gy, slots, (float(z_step), float(x_step)),
            (float(cx * x_step), float(cy * z_step))),
        out_shape=(
            jax.ShapeDtypeStruct((ROWS, 128), jnp.float32),
            jax.ShapeDtypeStruct(body_force.shape, jnp.float32),
        ),
        in_specs=[vmem] * 7,
        out_specs=(vmem, vmem),
        scratch_shapes=[
            pltpu.VMEM((7 if nodes <= 1024 else 6, nodes, nodes), jnp.bfloat16),
            pltpu.VMEM((cx, cy, cz), jnp.float32),
            pltpu.VMEM((COMP, cx + 2, cy, cz), jnp.float32),
            pltpu.VMEM((4, COMP, cy, cz), jnp.float32),
            pltpu.VMEM((2, 4, COMP, cy, cz), jnp.float32),
            pltpu.VMEM((8, nodes), jnp.float32),
            pltpu.VMEM((ITERS + 1, 4, 8, nodes), jnp.float32),
            pltpu.VMEM((8, 128), jnp.float32),
            pltpu.VMEM((ITERS, groups, 8, 128), jnp.float32),
            pltpu.VMEM((8, 128), jnp.float32),
            pltpu.VMEM((ITERS, rows_gy, 8, 128), jnp.float32),
            pltpu.VMEM((ROWS, 128), jnp.float32),
            pltpu.VMEM((groups, ROWS, 128), jnp.float32),
            pltpu.SemaphoreType.DMA((2, 2, 4)),
            pltpu.SemaphoreType.DMA((2, groups)),
            pltpu.SemaphoreType.DMA((2, ITERS + 1, 4)),
            pltpu.SemaphoreType.DMA((2, ITERS, groups)),
            pltpu.SemaphoreType.DMA((2, ITERS, rows_gy)),
        ],
        compiler_params=pltpu.CompilerParams(
            collective_id=0, has_side_effects=True,
            vmem_limit_bytes=(46 << 20) if nodes <= 1024 else (63 << 20)),
    )(
        body_force, shift_coef, jnp.broadcast_to(ids[None], (8, nodes)), ids[:, None], place, blocks, gap,
    )

    column = lax.rem(lax.axis_index("gx") - owners + groups, groups) * CAP + rank_in
    pick = (jnp.arange(128, dtype=jnp.int32)[:, None] == column[None, :]).astype(jnp.float32)
    multipliers = jnp.dot(multi[:MULT], pick, precision=lax.Precision.HIGHEST)
    return (multipliers, velocity)


def solution(mesh):
    in_specs = (
        P(None, "gx", "gy", None),
        P("gx", "gy", None),
        P(None, ("gx", "gy")),
        P(None, ("gx", "gy")),
        P(None, ("gx", "gy")),
        P(("gx", "gy"), None),
    )
    out_specs = (P(None, ("gx", "gy")), P(None, "gx", "gy", None))
    return jax.shard_map(shards, mesh=mesh, in_specs=in_specs, out_specs=out_specs, check_vma=False)
```

```python
import functools
import jax
import jax.numpy as jnp
from jax import lax
from jax.experimental import pallas as pl
from jax.experimental.pallas import tpu as pltpu
from jax.sharding import PartitionSpec as P

COMP = 3
NODES = 32
MULT = 81
ITERS = 4
CAP = 4
ROWS = 88
MESH = pl.DeviceIdType.MESH


def pieces(values):
    high = values.astype(jnp.bfloat16).astype(jnp.float32)
    return jnp.concatenate([high, values - high], axis=0).astype(jnp.bfloat16)


def uzawa_kernel(ngx, ngy, slots, strides, spans, force_ref, shift_ref, row_ref, col_ref,
                 place_ref, block_ref, gap_ref, mult_ref, out_ref, links, inv, grown, edge, face, sent, got, part,
                 line, total, far, own, home, face_sem, home_sem, swap_sem, line_sem, far_sem):
    me_x, me_y = lax.axis_index("gx"), lax.axis_index("gy")
    nodes = row_ref.shape[1]
    quads = nodes // 128
    z_step, x_step = strides
    x_span, y_span = spans

    barrier = pltpu.get_barrier_semaphore()
    for o in range(1, ngx):
        pl.semaphore_signal(barrier, inc=1, device_id={"gx": lax.rem(me_x + o, ngx)}, device_id_type=MESH)
    for o in range(1, ngy):
        pl.semaphore_signal(barrier, inc=1, device_id={"gy": lax.rem(me_y + o, ngy)}, device_id_type=MESH)
    pl.semaphore_wait(barrier, ngx + ngy - 2)

    def exchange(source, slot):
        copies = []
        for side, (axis, me, count, step) in enumerate(
            (("gx", me_x, ngx, 1), ("gx", me_x, ngx, ngx - 1), ("gy", me_y, ngy, 1), ("gy", me_y, ngy, ngy - 1))
        ):
            copy = pltpu.make_async_remote_copy(
                src_ref=source, dst_ref=got.at[slot, side],
                send_sem=swap_sem.at[0, slot, side], recv_sem=swap_sem.at[1, slot, side],
                device_id={axis: lax.rem(me + step, count)}, device_id_type=MESH)
            copy.start()
            copies.append(copy)
        return copies

    _, cx, cy, cz = force_ref.shape
    columns = cx * cy
    spot = links.shape[0] - 1

    def start_faces(time):
        for c in range(COMP):
            edge[0, c] = grown[c, cx]
            edge[1, c] = grown[c, 1]
            edge[2, c] = grown[c, 1:cx + 1, cy - 1, :]
            edge[3, c] = grown[c, 1:cx + 1, 0, :]
        copies = []
        for side, (axis, me, count, step) in enumerate(
            (("gx", me_x, ngx, 1), ("gx", me_x, ngx, ngx - 1), ("gy", me_y, ngy, 1), ("gy", me_y, ngy, ngy - 1))
        ):
            copy = pltpu.make_async_remote_copy(
                src_ref=edge.at[side], dst_ref=face.at[time, side],
                send_sem=face_sem.at[0, time, side], recv_sem=face_sem.at[1, time, side],
                device_id={axis: lax.rem(me + step, count)}, device_id_type=MESH)
            copy.start()
            copies.append(copy)
        return copies

    def finish_smooth(copies, time):
        for copy in copies:
            copy.wait()
        for c in range(COMP):
            grown[c, 0] = jnp.where(me_x > 0, face[time, 0, c], 0.0)
            grown[c, cx + 1] = jnp.where(me_x < ngx - 1, face[time, 1, c], 0.0)
        y_at = lax.broadcasted_iota(jnp.int32, (cy, cz), 0)
        z_at = lax.broadcasted_iota(jnp.int32, (cy, cz), 1)

        @pl.loop(0, cx)
        def _(x):
            scale = inv[x]
            for c in range(COMP):
                mid = grown[c, x + 1]
                low = jnp.where(me_y > 0, face[time, 2, c, pl.ds(x, 1), :], 0.0)
                high = jnp.where(me_y < ngy - 1, face[time, 3, c, pl.ds(x, 1), :], 0.0)
                beside = grown[c, x] + grown[c, x + 2]
                beside = beside + jnp.where(y_at == 0, low, pltpu.roll(mid, 1, 0))
                beside = beside + jnp.where(y_at == cy - 1, high, pltpu.roll(mid, cy - 1, 0))
                beside = beside + jnp.where(z_at == 0, 0.0, pltpu.roll(mid, 1, 1))
                beside = beside + jnp.where(z_at == cz - 1, 0.0, pltpu.roll(mid, cz - 1, 1))
                out_ref[c, x] = mid + beside * scale

    def mark_spots():
        @pl.loop(0, columns // 128)
        def _(i):
            at = pl.multiple_of(i * 128, 128)
            here = lax.broadcasted_iota(jnp.int32, (128, nodes), 0) + at
            links[spot, pl.ds(at, 128), :] = jnp.where(here == place_ref[0:1, :], 1.0, 0.0).astype(jnp.bfloat16)

    def gather(field):
        high = field.astype(jnp.bfloat16).astype(jnp.float32)
        both = jnp.concatenate([high, field - high], axis=1).astype(jnp.bfloat16)
        picked = lax.dot_general(
            both, links[spot, 0:columns, :], (((0,), (0,)), ((), ())), preferred_element_type=jnp.float32)
        z_row = lax.broadcasted_iota(jnp.int32, (cz, nodes), 0) == place_ref[1:2, :]
        return jnp.sum(jnp.where(z_row, picked[:cz] + picked[cz:], 0.0), axis=0, keepdims=True)

    def scatter(values):
        high = values.astype(jnp.bfloat16).astype(jnp.float32)
        z_row = lax.broadcasted_iota(jnp.int32, (cz, nodes), 0) == place_ref[1:2, :]
        both = jnp.concatenate(
            [jnp.where(z_row, high, 0.0), jnp.where(z_row, values - high, 0.0)], axis=0).astype(jnp.bfloat16)
        summed = lax.dot_general(
            links[spot, 0:columns, :], both, (((1,), (1,)), ((), ())), preferred_element_type=jnp.float32)
        return (summed[:, :cz] + summed[:, cz:]).reshape(cx, cy, cz)

    inv[...] = 1.0 / (6.0 + shift_ref[...])
    for c in range(COMP):
        grown[c, 1:cx + 1] = force_ref[c] * inv[...]
    faces = start_faces(0)
    copies = exchange(row_ref, 0)
    tile = 128
    mark_spots()

    @pl.loop(0, nodes // tile)
    def _(i):
        at = pl.ds(pl.multiple_of(i * tile, tile), tile)
        gap = jnp.abs(row_ref[0:1, :] - col_ref[at, :])
        links[0, at, :] = jnp.where(gap == 0.0, 1.0, 0.0).astype(jnp.bfloat16)
        links[1, at, :] = jnp.where(
            (gap == 1.0) | (gap == z_step) | (gap == x_step), 1.0, 0.0).astype(jnp.bfloat16)

    finish_smooth(faces, 0)
    sent[...] = jnp.zeros_like(sent)
    part[...] = jnp.zeros_like(part)
    for c in range(COMP):
        sent[c:c + 1, :] = gather(out_ref[c].reshape(columns, cz))
    inverse = gather(inv[...].reshape(columns, cz))
    start = sent[...]

    for copy in copies:
        copy.wait()
    nowhere = jnp.float32(8.0 * (x_span + x_step))
    from_left = jnp.where(me_x > 0, x_step - x_span, nowhere).astype(jnp.float32)
    from_right = jnp.where(me_x < ngx - 1, x_span - x_step, nowhere).astype(jnp.float32)
    from_below = jnp.where(me_y > 0, z_step - y_span, nowhere).astype(jnp.float32)
    from_above = jnp.where(me_y < ngy - 1, y_span - z_step, nowhere).astype(jnp.float32)

    @pl.loop(0, nodes // tile)
    def _(i):
        at = pl.ds(pl.multiple_of(i * tile, tile), tile)
        own = col_ref[at, :]
        for side, offset in enumerate((from_left, from_right, from_below, from_above)):
            moved = got[0, side, 0:1, :] + offset
            links[2 + side, at, :] = jnp.where(moved == own, 1.0, 0.0).astype(jnp.bfloat16)

    def apply_link(kind, values):
        both = lax.dot_general(
            pieces(values), links[kind], (((1,), (1,)), ((), ())), preferred_element_type=jnp.float32)
        return both[0:8] + both[8:16]

    def apply_bt(multi, into):
        for c in range(COMP):
            for q in range(quads):
                into[c:c + 1, q * 128:(q + 1) * 128] = jnp.sum(
                    block_ref[c * quads + q] * multi, axis=0, keepdims=True)

    def apply_b(values):
        image = jnp.zeros((ROWS, 128), jnp.float32)
        for c in range(COMP):
            for q in range(quads):
                image = image + block_ref[c * quads + q] * values[c:c + 1, q * 128:(q + 1) * 128]
        shift = 64
        while shift >= slots:
            image = image + pltpu.roll(image, shift, 1)
            shift //= 2
        return image

    def send_part(slot, stage):
        axis, me, count, source, room, sems = (
            ("gx", me_x, ngx, part, line, line_sem), ("gy", me_y, ngy, total, far, far_sem))[stage]
        copies = []
        for o in range(1, count):
            copy = pltpu.make_async_remote_copy(
                src_ref=source, dst_ref=room.at[slot, o],
                send_sem=sems.at[0, slot, o], recv_sem=sems.at[1, slot, o],
                device_id={axis: lax.rem(me + o, count)}, device_id_type=MESH)
            copy.start()
            copies.append(copy)
        return copies

    def add_parts(copies, slot, stage):
        source, room = ((part, line), (total, far))[stage]
        summed = source[...]
        for o, copy in enumerate(copies):
            copy.wait()
            summed = summed + room[slot, o + 1]
        return summed

    def start_image(field, slot):
        apply_bt(field, sent)
        scaled = sent[...] * inverse
        sent[...] = scaled
        return scaled, exchange(sent, slot)

    def local_image(scaled):
        return apply_link(0, scaled), apply_link(1, scaled)

    def finish_image(copies, slot, here, beside):
        for side, copy in enumerate(copies):
            copy.wait()
            beside = beside + apply_link(2 + side, got[slot, side])
        return apply_b(here + beside * inverse)

    def form_part(residual, direction, image):
        for row, (a, b) in enumerate(
            ((residual, residual), (direction, image), (residual, image), (image, image))):
            part[row:row + 1, :] = jnp.sum(a * b, axis=0, keepdims=True)

    def coefficients(tile_sum):
        sums = jnp.sum(tile_sum, axis=1, keepdims=True)
        norm_now, bend, cross, square = sums[0:1], sums[1:2], sums[2:3], sums[3:4]
        step_size = norm_now / bend
        norm_next = norm_now - 2.0 * step_size * cross + step_size * step_size * square
        return step_size, norm_next / norm_now

    def step(iteration, state):
        multi, residual, direction, image, reach = state
        form_part(residual, direction, image)
        parts = send_part(iteration, 0)
        scaled, copies = start_image(image, iteration + 2)
        here, beside = local_image(scaled)
        total[...] = add_parts(parts, iteration, 0)
        parts = send_part(iteration, 1)
        second = finish_image(copies, iteration + 2, here, beside)
        step_size, ratio = coefficients(add_parts(parts, iteration, 1))
        multi = multi + step_size * direction
        residual = residual - step_size * image
        reach = reach - step_size * second
        direction = residual + ratio * direction
        image = reach + ratio * image
        return multi, residual, direction, image, reach

    goal = apply_b(start) - gap_ref[...]
    scaled, copies = start_image(goal, 1)
    here, beside = local_image(scaled)
    image = finish_image(copies, 1, here, beside)
    multi, residual, direction, image, _ = lax.fori_loop(
        0, ITERS - 1, step, (jnp.zeros_like(goal), goal, goal, image, image))
    form_part(residual, direction, image)
    total[...] = add_parts(send_part(ITERS - 1, 0), ITERS - 1, 0)
    step_size, _ = coefficients(add_parts(send_part(ITERS - 1, 1), ITERS - 1, 1))
    multi = multi + step_size * direction
    own[...] = multi
    returns = []
    for o in range(1, ngx):
        copy = pltpu.make_async_remote_copy(
            src_ref=own, dst_ref=home.at[o], send_sem=home_sem.at[0, o], recv_sem=home_sem.at[1, o],
            device_id={"gx": lax.rem(me_x + o, ngx)}, device_id_type=MESH)
        copy.start()
        returns.append(copy)
    apply_bt(multi, sent)
    if spot < 6:
        mark_spots()
    for c in range(COMP):
        grown[c, 1:cx + 1] = (force_ref[c] - scatter(sent[c:c + 1, :])) * inv[...]
    finish_smooth(start_faces(1), 1)
    lane = lax.broadcasted_iota(jnp.int32, (ROWS, 128), 1) // CAP
    collected = jnp.zeros((ROWS, 128), jnp.float32)
    for o in range(ngx):
        if o:
            returns[o - 1].wait()
        tile_of = home[o] if o else own[...]
        turned = pltpu.roll(tile_of, lax.rem(o * CAP + 128 - me_x * CAP, 128), 1)
        collected = jnp.where(lane == o, turned, collected)
    mult_ref[...] = collected


def move_kernel(count, from_ref, to_ref, send_sem, recv_sem):
    me = lax.axis_index("gx")
    barrier = pltpu.get_barrier_semaphore()
    for o in range(1, count):
        pl.semaphore_signal(barrier, inc=1, device_id={"gx": lax.rem(me + o, count)}, device_id_type=MESH)
    pl.semaphore_wait(barrier, count - 1)
    copies = []
    for o in range(1, count):
        peer = lax.rem(me + o, count)
        copy = pltpu.make_async_remote_copy(
            src_ref=from_ref.at[peer], dst_ref=to_ref.at[me], send_sem=send_sem.at[o], recv_sem=recv_sem.at[o],
            device_id={"gx": peer}, device_id_type=MESH)
        copy.start()
        copies.append(copy)
    to_ref[me] = from_ref[me]
    for copy in copies:
        copy.wait()


def shards(body_force, shift_coef, coupling, node_cells, target_gap, new_owner):
    groups, rows_gy = lax.axis_size("gx"), lax.axis_size("gy")
    slots = groups * CAP
    pack = 128 // slots
    quads = NODES // pack
    nodes = NODES * slots
    owners = new_owner[:, 0]
    onehot = (owners[:, None] == jnp.arange(groups, dtype=jnp.int32)[None, :]).astype(jnp.int32)
    rank_in = jnp.sum((jnp.cumsum(onehot, axis=0) - 1) * onehot, axis=1)
    slot_of = owners * CAP + rank_in
    _, cx, cy, cz = body_force.shape
    cell_total = cx * cy * cz

    held = jnp.concatenate([coupling, node_cells.astype(jnp.float32), target_gap], axis=0)
    choose = (slot_of[:, None] == jnp.arange(slots, dtype=jnp.int32)[None, :]).astype(jnp.float32)
    held = jnp.dot(held, choose, precision=lax.Precision.HIGHEST)
    parted = held.T.reshape(groups, CAP, held.shape[0])
    moved = pl.pallas_call(
        functools.partial(move_kernel, groups),
        out_shape=jax.ShapeDtypeStruct(parted.shape, jnp.float32),
        in_specs=[pl.BlockSpec(memory_space=pltpu.VMEM)],
        out_specs=pl.BlockSpec(memory_space=pltpu.VMEM),
        scratch_shapes=[pltpu.SemaphoreType.DMA((groups,)), pltpu.SemaphoreType.DMA((groups,))],
        compiler_params=pltpu.CompilerParams(
            collective_id=1, has_side_effects=True, vmem_limit_bytes=24 << 20),
    )(parted)
    moved = moved.reshape(slots, held.shape[0]).T
    block_rows = COMP * NODES * MULT
    blocks = moved[:block_rows].reshape(COMP * quads, pack, MULT, slots)
    blocks = jnp.pad(blocks.transpose(0, 2, 1, 3).reshape(COMP * quads, MULT, 128), ((0, 0), (0, ROWS - MULT), (0, 0)))
    cell_int = jnp.round(moved[block_rows:block_rows + NODES]).astype(jnp.int32).reshape(nodes)
    gap = moved[block_rows + NODES:]

    z_step = cz + 2
    x_step = z_step * (3 * cy + 4)
    ids = (cell_int // (cy * cz) * x_step + cell_int // cz % cy * z_step + cell_int % cz).astype(jnp.float32)
    gap = jnp.tile(jnp.pad(gap, ((0, ROWS - MULT), (0, 0))), (1, pack))
    place = jnp.pad(jnp.stack([cell_int // cz, cell_int % cz]), ((0, 6), (0, 0)))

    vmem = pl.BlockSpec(memory_space=pltpu.VMEM)
    multi, velocity = pl.pallas_call(
        functools.partial(
            uzawa_kernel, groups, rows_gy, slots, (float(z_step), float(x_step)),
            (float(cx * x_step), float(cy * z_step))),
        out_shape=(
            jax.ShapeDtypeStruct((ROWS, 128), jnp.float32),
            jax.ShapeDtypeStruct(body_force.shape, jnp.float32),
        ),
        in_specs=[vmem] * 7,
        out_specs=(vmem, vmem),
        scratch_shapes=[
            pltpu.VMEM((7 if nodes <= 1024 else 6, nodes, nodes), jnp.bfloat16),
            pltpu.VMEM((cx, cy, cz), jnp.float32),
            pltpu.VMEM((COMP, cx + 2, cy, cz), jnp.float32),
            pltpu.VMEM((4, COMP, cy, cz), jnp.float32),
            pltpu.VMEM((2, 4, COMP, cy, cz), jnp.float32),
            pltpu.VMEM((8, nodes), jnp.float32),
            pltpu.VMEM((ITERS + 1, 4, 8, nodes), jnp.float32),
            pltpu.VMEM((8, 128), jnp.float32),
            pltpu.VMEM((ITERS, groups, 8, 128), jnp.float32),
            pltpu.VMEM((8, 128), jnp.float32),
            pltpu.VMEM((ITERS, rows_gy, 8, 128), jnp.float32),
            pltpu.VMEM((ROWS, 128), jnp.float32),
            pltpu.VMEM((groups, ROWS, 128), jnp.float32),
            pltpu.SemaphoreType.DMA((2, 2, 4)),
            pltpu.SemaphoreType.DMA((2, groups)),
            pltpu.SemaphoreType.DMA((2, ITERS + 1, 4)),
            pltpu.SemaphoreType.DMA((2, ITERS, groups)),
            pltpu.SemaphoreType.DMA((2, ITERS, rows_gy)),
        ],
        compiler_params=pltpu.CompilerParams(
            collective_id=0, has_side_effects=True,
            vmem_limit_bytes=(46 << 20) if nodes <= 1024 else (63 << 20)),
    )(
        body_force, shift_coef, jnp.broadcast_to(ids[None], (8, nodes)), ids[:, None], place, blocks, gap,
    )

    column = lax.rem(lax.axis_index("gx") - owners + groups, groups) * CAP + rank_in
    pick = (jnp.arange(128, dtype=jnp.int32)[:, None] == column[None, :]).astype(jnp.float32)
    multipliers = jnp.dot(multi[:MULT], pick, precision=lax.Precision.HIGHEST)
    return (multipliers, velocity)


def solution(mesh):
    in_specs = (
        P(None, "gx", "gy", None),
        P("gx", "gy", None),
        P(None, ("gx", "gy")),
        P(None, ("gx", "gy")),
        P(None, ("gx", "gy")),
        P(("gx", "gy"), None),
    )
    out_specs = (P(None, ("gx", "gy")), P(None, "gx", "gy", None))
    return jax.shard_map(shards, mesh=mesh, in_specs=in_specs, out_specs=out_specs, check_vma=False)
```

```python
import functools
import jax
import jax.numpy as jnp
from jax import lax
from jax.experimental import pallas as pl
from jax.experimental.pallas import tpu as pltpu
from jax.sharding import PartitionSpec as P

COMP = 3
NODES = 32
MULT = 81
ITERS = 4
CAP = 4
ROWS = 88
MESH = pl.DeviceIdType.MESH


def pieces(values):
    high = values.astype(jnp.bfloat16).astype(jnp.float32)
    return jnp.concatenate([high, values - high], axis=0).astype(jnp.bfloat16)


def uzawa_kernel(ngx, ngy, slots, strides, spans, force_ref, shift_ref, row_ref, col_ref,
                 place_ref, block_ref, gap_ref, mult_ref, out_ref, links, inv, grown, edge, face, sent, got, part,
                 line, total, far, own, home, face_sem, home_sem, swap_sem, line_sem, far_sem):
    me_x, me_y = lax.axis_index("gx"), lax.axis_index("gy")
    nodes = row_ref.shape[1]
    quads = nodes // 128
    z_step, x_step = strides
    x_span, y_span = spans

    barrier = pltpu.get_barrier_semaphore()
    for o in range(1, ngx):
        pl.semaphore_signal(barrier, inc=1, device_id={"gx": lax.rem(me_x + o, ngx)}, device_id_type=MESH)
    for o in range(1, ngy):
        pl.semaphore_signal(barrier, inc=1, device_id={"gy": lax.rem(me_y + o, ngy)}, device_id_type=MESH)
    pl.semaphore_wait(barrier, ngx + ngy - 2)

    def exchange(source, slot):
        copies = []
        for side, (axis, me, count, step) in enumerate(
            (("gx", me_x, ngx, 1), ("gx", me_x, ngx, ngx - 1), ("gy", me_y, ngy, 1), ("gy", me_y, ngy, ngy - 1))
        ):
            copy = pltpu.make_async_remote_copy(
                src_ref=source, dst_ref=got.at[slot, side],
                send_sem=swap_sem.at[0, slot, side], recv_sem=swap_sem.at[1, slot, side],
                device_id={axis: lax.rem(me + step, count)}, device_id_type=MESH)
            copy.start()
            copies.append(copy)
        return copies

    _, cx, cy, cz = force_ref.shape
    columns = cx * cy
    spot = links.shape[0] - 1

    def start_faces(time):
        for c in range(COMP):
            edge[0, c] = grown[c, cx]
            edge[1, c] = grown[c, 1]
            edge[2, c] = grown[c, 1:cx + 1, cy - 1, :]
            edge[3, c] = grown[c, 1:cx + 1, 0, :]
        copies = []
        for side, (axis, me, count, step) in enumerate(
            (("gx", me_x, ngx, 1), ("gx", me_x, ngx, ngx - 1), ("gy", me_y, ngy, 1), ("gy", me_y, ngy, ngy - 1))
        ):
            copy = pltpu.make_async_remote_copy(
                src_ref=edge.at[side], dst_ref=face.at[time, side],
                send_sem=face_sem.at[0, time, side], recv_sem=face_sem.at[1, time, side],
                device_id={axis: lax.rem(me + step, count)}, device_id_type=MESH)
            copy.start()
            copies.append(copy)
        return copies

    def finish_smooth(copies, time):
        for copy in copies:
            copy.wait()
        for c in range(COMP):
            grown[c, 0] = jnp.where(me_x > 0, face[time, 0, c], 0.0)
            grown[c, cx + 1] = jnp.where(me_x < ngx - 1, face[time, 1, c], 0.0)
        y_at = lax.broadcasted_iota(jnp.int32, (cy, cz), 0)
        z_at = lax.broadcasted_iota(jnp.int32, (cy, cz), 1)

        @pl.loop(0, cx, unroll=4)
        def _(x):
            scale = inv[x]
            for c in range(COMP):
                mid = grown[c, x + 1]
                low = jnp.where(me_y > 0, face[time, 2, c, pl.ds(x, 1), :], 0.0)
                high = jnp.where(me_y < ngy - 1, face[time, 3, c, pl.ds(x, 1), :], 0.0)
                beside = grown[c, x] + grown[c, x + 2]
                beside = beside + jnp.where(y_at == 0, low, pltpu.roll(mid, 1, 0))
                beside = beside + jnp.where(y_at == cy - 1, high, pltpu.roll(mid, cy - 1, 0))
                beside = beside + jnp.where(z_at == 0, 0.0, pltpu.roll(mid, 1, 1))
                beside = beside + jnp.where(z_at == cz - 1, 0.0, pltpu.roll(mid, cz - 1, 1))
                out_ref[c, x] = mid + beside * scale

    def mark_spots():
        @pl.loop(0, columns // 128, unroll=2)
        def _(i):
            at = pl.multiple_of(i * 128, 128)
            here = lax.broadcasted_iota(jnp.int32, (128, nodes), 0) + at
            links[spot, pl.ds(at, 128), :] = jnp.where(here == place_ref[0:1, :], 1.0, 0.0).astype(jnp.bfloat16)

    def gather(field):
        high = field.astype(jnp.bfloat16).astype(jnp.float32)
        both = jnp.concatenate([high, field - high], axis=1).astype(jnp.bfloat16)
        picked = lax.dot_general(
            both, links[spot, 0:columns, :], (((0,), (0,)), ((), ())), preferred_element_type=jnp.float32)
        z_row = lax.broadcasted_iota(jnp.int32, (cz, nodes), 0) == place_ref[1:2, :]
        return jnp.sum(jnp.where(z_row, picked[:cz] + picked[cz:], 0.0), axis=0, keepdims=True)

    def scatter(values):
        high = values.astype(jnp.bfloat16).astype(jnp.float32)
        z_row = lax.broadcasted_iota(jnp.int32, (cz, nodes), 0) == place_ref[1:2, :]
        both = jnp.concatenate(
            [jnp.where(z_row, high, 0.0), jnp.where(z_row, values - high, 0.0)], axis=0).astype(jnp.bfloat16)
        summed = lax.dot_general(
            links[spot, 0:columns, :], both, (((1,), (1,)), ((), ())), preferred_element_type=jnp.float32)
        return (summed[:, :cz] + summed[:, cz:]).reshape(cx, cy, cz)

    inv[...] = 1.0 / (6.0 + shift_ref[...])
    for c in range(COMP):
        grown[c, 1:cx + 1] = force_ref[c] * inv[...]
    faces = start_faces(0)
    copies = exchange(row_ref, 0)
    tile = 128
    mark_spots()

    @pl.loop(0, nodes // tile, unroll=2)
    def _(i):
        at = pl.ds(pl.multiple_of(i * tile, tile), tile)
        gap = jnp.abs(row_ref[0:1, :] - col_ref[at, :])
        links[0, at, :] = jnp.where(gap == 0.0, 1.0, 0.0).astype(jnp.bfloat16)
        links[1, at, :] = jnp.where(
            (gap == 1.0) | (gap == z_step) | (gap == x_step), 1.0, 0.0).astype(jnp.bfloat16)

    finish_smooth(faces, 0)
    sent[...] = jnp.zeros_like(sent)
    part[...] = jnp.zeros_like(part)
    for c in range(COMP):
        sent[c:c + 1, :] = gather(out_ref[c].reshape(columns, cz))
    inverse = gather(inv[...].reshape(columns, cz))
    start = sent[...]

    for copy in copies:
        copy.wait()
    nowhere = jnp.float32(8.0 * (x_span + x_step))
    from_left = jnp.where(me_x > 0, x_step - x_span, nowhere).astype(jnp.float32)
    from_right = jnp.where(me_x < ngx - 1, x_span - x_step, nowhere).astype(jnp.float32)
    from_below = jnp.where(me_y > 0, z_step - y_span, nowhere).astype(jnp.float32)
    from_above = jnp.where(me_y < ngy - 1, y_span - z_step, nowhere).astype(jnp.float32)

    @pl.loop(0, nodes // tile, unroll=2)
    def _(i):
        at = pl.ds(pl.multiple_of(i * tile, tile), tile)
        own = col_ref[at, :]
        for side, offset in enumerate((from_left, from_right, from_below, from_above)):
            moved = got[0, side, 0:1, :] + offset
            links[2 + side, at, :] = jnp.where(moved == own, 1.0, 0.0).astype(jnp.bfloat16)

    def apply_link(kind, values):
        both = lax.dot_general(
            pieces(values), links[kind], (((1,), (1,)), ((), ())), preferred_element_type=jnp.float32)
        return both[0:8] + both[8:16]

    def apply_bt(multi, into):
        for c in range(COMP):
            for q in range(quads):
                into[c:c + 1, q * 128:(q + 1) * 128] = jnp.sum(
                    block_ref[c * quads + q] * multi, axis=0, keepdims=True)

    def apply_b(values):
        image = jnp.zeros((ROWS, 128), jnp.float32)
        for c in range(COMP):
            for q in range(quads):
                image = image + block_ref[c * quads + q] * values[c:c + 1, q * 128:(q + 1) * 128]
        shift = 64
        while shift >= slots:
            image = image + pltpu.roll(image, shift, 1)
            shift //= 2
        return image

    def send_part(slot, stage):
        axis, me, count, source, room, sems = (
            ("gx", me_x, ngx, part, line, line_sem), ("gy", me_y, ngy, total, far, far_sem))[stage]
        copies = []
        for o in range(1, count):
            copy = pltpu.make_async_remote_copy(
                src_ref=source, dst_ref=room.at[slot, o],
                send_sem=sems.at[0, slot, o], recv_sem=sems.at[1, slot, o],
                device_id={axis: lax.rem(me + o, count)}, device_id_type=MESH)
            copy.start()
            copies.append(copy)
        return copies

    def add_parts(copies, slot, stage):
        source, room = ((part, line), (total, far))[stage]
        summed = source[...]
        for o, copy in enumerate(copies):
            copy.wait()
            summed = summed + room[slot, o + 1]
        return summed

    def start_image(field, slot):
        apply_bt(field, sent)
        scaled = sent[...] * inverse
        sent[...] = scaled
        return scaled, exchange(sent, slot)

    def local_image(scaled):
        return apply_link(0, scaled), apply_link(1, scaled)

    def finish_image(copies, slot, here, beside):
        for side, copy in enumerate(copies):
            copy.wait()
            beside = beside + apply_link(2 + side, got[slot, side])
        return apply_b(here + beside * inverse)

    def form_part(residual, direction, image):
        for row, (a, b) in enumerate(
            ((residual, residual), (direction, image), (residual, image), (image, image))):
            part[row:row + 1, :] = jnp.sum(a * b, axis=0, keepdims=True)

    def coefficients(tile_sum):
        sums = jnp.sum(tile_sum, axis=1, keepdims=True)
        norm_now, bend, cross, square = sums[0:1], sums[1:2], sums[2:3], sums[3:4]
        step_size = norm_now / bend
        norm_next = norm_now - 2.0 * step_size * cross + step_size * step_size * square
        return step_size, norm_next / norm_now

    def step(iteration, state):
        multi, residual, direction, image, reach = state
        form_part(residual, direction, image)
        parts = send_part(iteration, 0)
        scaled, copies = start_image(image, iteration + 2)
        here, beside = local_image(scaled)
        total[...] = add_parts(parts, iteration, 0)
        parts = send_part(iteration, 1)
        second = finish_image(copies, iteration + 2, here, beside)
        step_size, ratio = coefficients(add_parts(parts, iteration, 1))
        multi = multi + step_size * direction
        residual = residual - step_size * image
        reach = reach - step_size * second
        direction = residual + ratio * direction
        image = reach + ratio * image
        return multi, residual, direction, image, reach

    goal = apply_b(start) - gap_ref[...]
    scaled, copies = start_image(goal, 1)
    here, beside = local_image(scaled)
    image = finish_image(copies, 1, here, beside)
    multi, residual, direction, image, _ = lax.fori_loop(
        0, ITERS - 1, step, (jnp.zeros_like(goal), goal, goal, image, image))
    form_part(residual, direction, image)
    total[...] = add_parts(send_part(ITERS - 1, 0), ITERS - 1, 0)
    step_size, _ = coefficients(add_parts(send_part(ITERS - 1, 1), ITERS - 1, 1))
    multi = multi + step_size * direction
    own[...] = multi
    returns = []
    for o in range(1, ngx):
        copy = pltpu.make_async_remote_copy(
            src_ref=own, dst_ref=home.at[o], send_sem=home_sem.at[0, o], recv_sem=home_sem.at[1, o],
            device_id={"gx": lax.rem(me_x + o, ngx)}, device_id_type=MESH)
        copy.start()
        returns.append(copy)
    apply_bt(multi, sent)
    if spot < 6:
        mark_spots()
    for c in range(COMP):
        grown[c, 1:cx + 1] = (force_ref[c] - scatter(sent[c:c + 1, :])) * inv[...]
    finish_smooth(start_faces(1), 1)
    lane = lax.broadcasted_iota(jnp.int32, (ROWS, 128), 1) // CAP
    collected = jnp.zeros((ROWS, 128), jnp.float32)
    for o in range(ngx):
        if o:
            returns[o - 1].wait()
        tile_of = home[o] if o else own[...]
        turned = pltpu.roll(tile_of, lax.rem(o * CAP + 128 - me_x * CAP, 128), 1)
        collected = jnp.where(lane == o, turned, collected)
    mult_ref[...] = collected


def move_kernel(count, from_ref, to_ref, send_sem, recv_sem):
    me = lax.axis_index("gx")
    barrier = pltpu.get_barrier_semaphore()
    for o in range(1, count):
        pl.semaphore_signal(barrier, inc=1, device_id={"gx": lax.rem(me + o, count)}, device_id_type=MESH)
    pl.semaphore_wait(barrier, count - 1)
    copies = []
    for o in range(1, count):
        peer = lax.rem(me + o, count)
        copy = pltpu.make_async_remote_copy(
            src_ref=from_ref.at[peer], dst_ref=to_ref.at[me], send_sem=send_sem.at[o], recv_sem=recv_sem.at[o],
            device_id={"gx": peer}, device_id_type=MESH)
        copy.start()
        copies.append(copy)
    to_ref[me] = from_ref[me]
    for copy in copies:
        copy.wait()


def shards(body_force, shift_coef, coupling, node_cells, target_gap, new_owner):
    groups, rows_gy = lax.axis_size("gx"), lax.axis_size("gy")
    slots = groups * CAP
    pack = 128 // slots
    quads = NODES // pack
    nodes = NODES * slots
    owners = new_owner[:, 0]
    onehot = (owners[:, None] == jnp.arange(groups, dtype=jnp.int32)[None, :]).astype(jnp.int32)
    rank_in = jnp.sum((jnp.cumsum(onehot, axis=0) - 1) * onehot, axis=1)
    slot_of = owners * CAP + rank_in
    _, cx, cy, cz = body_force.shape
    cell_total = cx * cy * cz

    held = jnp.concatenate([coupling, node_cells.astype(jnp.float32), target_gap], axis=0)
    choose = (slot_of[:, None] == jnp.arange(slots, dtype=jnp.int32)[None, :]).astype(jnp.float32)
    held = jnp.dot(held, choose, precision=lax.Precision.HIGHEST)
    parted = held.T.reshape(groups, CAP, held.shape[0])
    moved = pl.pallas_call(
        functools.partial(move_kernel, groups),
        out_shape=jax.ShapeDtypeStruct(parted.shape, jnp.float32),
        in_specs=[pl.BlockSpec(memory_space=pltpu.VMEM)],
        out_specs=pl.BlockSpec(memory_space=pltpu.VMEM),
        scratch_shapes=[pltpu.SemaphoreType.DMA((groups,)), pltpu.SemaphoreType.DMA((groups,))],
        compiler_params=pltpu.CompilerParams(
            collective_id=1, has_side_effects=True, vmem_limit_bytes=24 << 20),
    )(parted)
    moved = moved.reshape(slots, held.shape[0]).T
    block_rows = COMP * NODES * MULT
    blocks = moved[:block_rows].reshape(COMP * quads, pack, MULT, slots)
    blocks = jnp.pad(blocks.transpose(0, 2, 1, 3).reshape(COMP * quads, MULT, 128), ((0, 0), (0, ROWS - MULT), (0, 0)))
    cell_int = jnp.round(moved[block_rows:block_rows + NODES]).astype(jnp.int32).reshape(nodes)
    gap = moved[block_rows + NODES:]

    z_step = cz + 2
    x_step = z_step * (3 * cy + 4)
    ids = (cell_int // (cy * cz) * x_step + cell_int // cz % cy * z_step + cell_int % cz).astype(jnp.float32)
    gap = jnp.tile(jnp.pad(gap, ((0, ROWS - MULT), (0, 0))), (1, pack))
    place = jnp.pad(jnp.stack([cell_int // cz, cell_int % cz]), ((0, 6), (0, 0)))

    vmem = pl.BlockSpec(memory_space=pltpu.VMEM)
    multi, velocity = pl.pallas_call(
        functools.partial(
            uzawa_kernel, groups, rows_gy, slots, (float(z_step), float(x_step)),
            (float(cx * x_step), float(cy * z_step))),
        out_shape=(
            jax.ShapeDtypeStruct((ROWS, 128), jnp.float32),
            jax.ShapeDtypeStruct(body_force.shape, jnp.float32),
        ),
        in_specs=[vmem] * 7,
        out_specs=(vmem, vmem),
        scratch_shapes=[
            pltpu.VMEM((7 if nodes <= 1024 else 6, nodes, nodes), jnp.bfloat16),
            pltpu.VMEM((cx, cy, cz), jnp.float32),
            pltpu.VMEM((COMP, cx + 2, cy, cz), jnp.float32),
            pltpu.VMEM((4, COMP, cy, cz), jnp.float32),
            pltpu.VMEM((2, 4, COMP, cy, cz), jnp.float32),
            pltpu.VMEM((8, nodes), jnp.float32),
            pltpu.VMEM((ITERS + 1, 4, 8, nodes), jnp.float32),
            pltpu.VMEM((8, 128), jnp.float32),
            pltpu.VMEM((ITERS, groups, 8, 128), jnp.float32),
            pltpu.VMEM((8, 128), jnp.float32),
            pltpu.VMEM((ITERS, rows_gy, 8, 128), jnp.float32),
            pltpu.VMEM((ROWS, 128), jnp.float32),
            pltpu.VMEM((groups, ROWS, 128), jnp.float32),
            pltpu.SemaphoreType.DMA((2, 2, 4)),
            pltpu.SemaphoreType.DMA((2, groups)),
            pltpu.SemaphoreType.DMA((2, ITERS + 1, 4)),
            pltpu.SemaphoreType.DMA((2, ITERS, groups)),
            pltpu.SemaphoreType.DMA((2, ITERS, rows_gy)),
        ],
        compiler_params=pltpu.CompilerParams(
            collective_id=0, has_side_effects=True,
            vmem_limit_bytes=(46 << 20) if nodes <= 1024 else (63 << 20)),
    )(
        body_force, shift_coef, jnp.broadcast_to(ids[None], (8, nodes)), ids[:, None], place, blocks, gap,
    )

    column = lax.rem(lax.axis_index("gx") - owners + groups, groups) * CAP + rank_in
    pick = (jnp.arange(128, dtype=jnp.int32)[:, None] == column[None, :]).astype(jnp.float32)
    multipliers = jnp.dot(multi[:MULT], pick, precision=lax.Precision.HIGHEST)
    return (multipliers, velocity)


def solution(mesh):
    in_specs = (
        P(None, "gx", "gy", None),
        P("gx", "gy", None),
        P(None, ("gx", "gy")),
        P(None, ("gx", "gy")),
        P(None, ("gx", "gy")),
        P(("gx", "gy"), None),
    )
    out_specs = (P(None, ("gx", "gy")), P(None, "gx", "gy", None))
    return jax.shard_map(shards, mesh=mesh, in_specs=in_specs, out_specs=out_specs, check_vma=False)
```
